512 devices in a mesh: scene: 8 (over x, core), img: 64 (over y, z).
Axes of the slice: x: 4, y: 8, z: 8, core: 2. Of those that a mesh axis runs over, the one named last changes fastest.
Arguments:
- tokens: bfloat16 [8, 64, 8, 768], P('scene', 'img'), may hold values from -6 to 6
- pair_list: int32 [8, 64, 16, 2], P('scene', 'img'), may hold values from 0 to 63, as said below
- pair_count: int32 [8, 64], P('scene', 'img'), may hold values from 8 to 16, as said below
- poses: float32 [8, 64, 12], P('scene'), may hold values from -1.5 to 1.5
- gain_query: float32 [768], replicated, may hold values from 0.3 to 3
- gain_kv: float32 [768], replicated, may hold values from 0.3 to 3
- w_query: bfloat16 [768, 384], P('scene'), may hold values from -0.21875 to 0.21875
- w_kv: bfloat16 [768, 768], P('scene'), may hold values from -0.21875 to 0.21875
- w_out: bfloat16 [384, 768], P('scene'), may hold values from -0.3125 to 0.3125
- w_head: bfloat16 [768, 1024], P('scene'), may hold values from -0.21875 to 0.21875
Outputs:
- joined_points: bfloat16 [8, 64, 3, 2048], P('scene', 'img')
- pose_grad: float32 [8, 64, 3], P('scene', 'img')
The draws below stay inside these ranges and needn't reach their ends.
Inputs may be any that keep to these rules, and one draw needn't show every extreme that they name: `pair_list`: indices are images of the owner's scene group; the two images of a pair differ; among the 16 slots of one device no image appears more than 1 times, and some device names one image 1 times; slot 0 of device d names image d first. `pair_count`: each device uses 16 slots or 8 of them; in every scene group some device uses all 16 slots.
All inputs are finite; a program needn't handle non-finite values.
Results may differ from the reference program's by a relative error of at most 0.034.
Values may be sent and summed in bfloat16 or wider, within the bound.
A program may use at most 64 MiB of HBM per device.

```python
import math
import jax
import jax.numpy as jnp
from jax import lax

D = 768
HEADS = 6
HEAD_DIM = 64
PIX = 256
TOK = 8
PAIR_DEV = 16
SCENES = 8
IMAGES = 64
CAP = 1


def draw_pair_list(key, part):
    key = jax.random.fold_in(key, 11)
    key_draws = jax.random.split(key, SCENES * IMAGES * CAP)
    shuffled = jax.vmap(lambda one_key: jax.random.permutation(one_key, IMAGES))(key_draws)
    shuffled = shuffled.reshape(SCENES, IMAGES, CAP, IMAGES).astype(jnp.int32)
    owners = jnp.arange(IMAGES, dtype=jnp.int32)[None, :, None]
    first_round = shuffled[:, :, 0, :]
    leading = first_round[:, :, :1]
    first_round = jnp.where(first_round == owners, leading, first_round)
    first_round = jnp.concatenate([jnp.broadcast_to(owners, (SCENES, IMAGES, 1)), first_round[:, :, 1:]], axis=2)
    rounds = jnp.concatenate([first_round[:, :, None, :], shuffled[:, :, 1:, :]], axis=2)
    view_list = rounds.reshape(SCENES, IMAGES, CAP * IMAGES)[:, :, :2 * PAIR_DEV]
    return view_list.reshape(SCENES, IMAGES, PAIR_DEV, 2).astype(jnp.int32)


def draw_pair_count(key, part):
    key = jax.random.fold_in(key, 12)
    key_shift, key_busy = jax.random.split(key)
    picks = jax.random.randint(key_shift, (SCENES, IMAGES), 0, 4)
    counts = jnp.where(picks == 0, jnp.maximum(PAIR_DEV // 2, 1), PAIR_DEV)
    busiest = jax.random.randint(key_busy, (SCENES, 1), 0, IMAGES)
    counts = jnp.where(jnp.arange(IMAGES)[None, :] == busiest, PAIR_DEV, counts)
    return counts.astype(jnp.int32)


def block_levels(key, extent, pieces, low, high):
    def one(axis_at, shards_of):
        heights = jax.random.uniform(jax.random.fold_in(jax.random.fold_in(key, 6), axis_at), (shards_of,), jnp.float32, low / len(pieces), high / len(pieces))
        return jnp.repeat(jnp.exp(heights), extent[axis_at] // shards_of).reshape((-1,) + (1,) * (len(extent) - axis_at - 1))

    factor_of = one(*pieces[0])
    for cut in pieces[1:]:
        factor_of = factor_of * one(*cut)
    return factor_of


def gaussian(rng, shape, deviation, bound, cuts=(), kind=jnp.bfloat16):
    factor_of = block_levels(rng, shape, cuts, -0.22, 0.18) if cuts else 1.0
    result = jax.random.normal(rng, shape, jnp.float32) * deviation * factor_of
    return jnp.minimum(jnp.maximum(result, -bound), bound).astype(kind)


def setup_inputs(seed: int = 0) -> dict:
    seeds = jax.random.split(jax.random.key(seed), 11)
    return {
        "tokens": gaussian(seeds[0], (SCENES, IMAGES, TOK, D), 1.0, 6.0, ((0, 8), (1, 64))),
        "pair_list": draw_pair_list(jax.random.fold_in(seeds[10], 71), 0),
        "pair_count": draw_pair_count(jax.random.fold_in(seeds[10], 71), 0),
        "poses": gaussian(seeds[3], (SCENES, IMAGES, 12), 0.3, 1.5, ((0, 8),), jnp.float32),
        "gain_query": jnp.clip(jnp.exp(jax.random.uniform(seeds[4], (D,), jnp.float32, math.log(0.3), math.log(3.0))), 0.3, 3.0),
        "gain_kv": jnp.clip(jnp.exp(jax.random.uniform(seeds[5], (D,), jnp.float32, math.log(0.3), math.log(3.0))), 0.3, 3.0),
        "w_query": gaussian(seeds[6], (D, HEADS * HEAD_DIM), D ** -0.5, 0.21875, ((0, 8),)),
        "w_kv": gaussian(seeds[7], (D, 2 * HEADS * HEAD_DIM), D ** -0.5, 0.21875, ((0, 8),)),
        "w_out": gaussian(seeds[8], (HEADS * HEAD_DIM, D), (HEADS * HEAD_DIM) ** -0.5, 0.3125, ((0, 8),)),
        "w_head": gaussian(seeds[9], (D, 4 * PIX), D ** -0.5, 0.21875, ((0, 8),)),
    }


def layer_norm(values_in, gain_vec):
    values_in = values_in.astype(jnp.float32)
    centered = values_in - lax.optimization_barrier(jnp.mean(values_in, axis=-1, keepdims=True))
    variance = lax.optimization_barrier(jnp.mean(centered * centered, axis=-1, keepdims=True))
    return centered * lax.rsqrt(variance + 1e-05) * gain_vec

def decode_views(view_tokens, gain_query, gain_kv, w_query, w_kv, w_out):
    view_count = view_tokens.shape[0]
    flat_rows = view_tokens.reshape(view_count * TOK, D)
    normed = layer_norm(flat_rows, gain_query).astype(jnp.bfloat16)
    queries = jnp.dot(normed, w_query, preferred_element_type=jnp.float32).astype(jnp.bfloat16)
    normed = layer_norm(flat_rows, gain_kv).astype(jnp.bfloat16)
    key_value = jnp.dot(normed, w_kv, preferred_element_type=jnp.float32).astype(jnp.bfloat16)
    key_value = jnp.flip(key_value.reshape(view_count // 2, 2, TOK, 2 * HEADS * HEAD_DIM), axis=1)
    key_value = key_value.reshape(view_count, TOK, 2, HEADS, HEAD_DIM)
    queries = queries.reshape(view_count, TOK, HEADS, HEAD_DIM)
    scores = jnp.einsum('vqhd,vkhd->vhqk', queries.astype(jnp.float32), key_value[:, :, 0].astype(jnp.float32))
    scores = scores * HEAD_DIM ** (-0.5)
    weights = jax.nn.softmax(scores, axis=-1).astype(jnp.bfloat16)
    attended = jnp.einsum('vhqk,vkhd->vqhd', weights.astype(jnp.float32), key_value[:, :, 1].astype(jnp.float32))
    attended = attended.astype(jnp.bfloat16).reshape(view_count * TOK, HEADS * HEAD_DIM)
    projected = jnp.dot(attended, w_out, preferred_element_type=jnp.float32)
    return (flat_rows.astype(jnp.float32) + projected).astype(jnp.bfloat16)

def point_head(decoded, w_head, pose_rows, in_use):
    view_count = pose_rows.shape[0]
    raw_out = jnp.dot(decoded, w_head, preferred_element_type=jnp.float32).reshape(view_count, TOK, 4, PIX)
    raw_out = jnp.transpose(raw_out, (0, 2, 1, 3)).reshape(view_count, 4, TOK * PIX)
    confidence = (1.0 + jnp.exp(raw_out[:, 3])) * in_use[:, None]
    rotation = jnp.eye(3, dtype=jnp.float32) + pose_rows[:, :9].reshape(view_count, 3, 3)
    world_pts = jnp.einsum('vij,vjp->vip', rotation, raw_out[:, :3], precision=lax.Precision.HIGHEST)
    return (confidence, world_pts + pose_rows[:, 9:, None])

def reference(tokens, pair_list, pair_count, poses, gain_query, gain_kv, w_query, w_kv, w_out, w_head):
    image_ids = jnp.arange(IMAGES).astype(jnp.int32)

    def scene_terms(inputs):
        tokens_s, pairs_s, counts_s, poses_s = inputs

        def owner_step(collected, rows):
            pair_rows, used_count = rows
            view_image = pair_rows.reshape(-1)
            in_use = jnp.repeat((jnp.arange(PAIR_DEV) < used_count).astype(jnp.float32), 2)
            first_image = jnp.repeat(pair_rows[:, 0], 2)
            decoded = decode_views(tokens_s[view_image], gain_query, gain_kv, w_query, w_kv, w_out)
            confidence, world_pts = point_head(decoded, w_head, poses_s[first_image], in_use)
            image_hot = (view_image[:, None] == image_ids[None, :]).astype(jnp.float32)
            weighted_pts = confidence[:, None] * world_pts
            numerator = collected[0] + jnp.einsum('vi,vcp->icp', image_hot, weighted_pts, precision=lax.Precision.HIGHEST)
            denominator = collected[1] + jnp.einsum('vi,vp->ip', image_hot, confidence, precision=lax.Precision.HIGHEST)
            return ((numerator, denominator), (confidence, lax.optimization_barrier(jnp.sum(weighted_pts, axis=2))))
        start = (jnp.zeros((IMAGES, 3, TOK * PIX), jnp.float32), jnp.zeros((IMAGES, TOK * PIX), jnp.float32))
        (numerator, denominator), (confidences, weighted_sums) = lax.scan(owner_step, start, (pairs_s, counts_s))
        joined = (numerator / denominator[:, None]).astype(jnp.bfloat16)

        def gradient_step(collected, rows):
            pair_rows, confidence, weighted = rows
            target = joined[pair_rows.reshape(-1)].astype(jnp.float32)
            residual_sum = weighted - lax.optimization_barrier(jnp.sum(confidence[:, None] * target, axis=2))
            per_pair = residual_sum.reshape(PAIR_DEV, 2, 3).sum(axis=1)
            owner_hot = (pair_rows[:, 0][:, None] == image_ids[None, :]).astype(jnp.float32)
            return (collected + jnp.einsum('ki,kc->ic', owner_hot, per_pair, precision=lax.Precision.HIGHEST), None)
        gradient, _ = lax.scan(gradient_step, jnp.zeros((IMAGES, 3), jnp.float32), (pairs_s, confidences, weighted_sums))
        return (joined, gradient * (2.0 / (TOK * PIX)))
    return lax.map(scene_terms, (tokens, pair_list, pair_count, poses))
```

```python
import jax
import jax.numpy as jnp
from jax import lax
from jax.experimental import pallas as pl
from jax.experimental.pallas import tpu as pltpu
from jax.sharding import PartitionSpec as P

D = 768
HALF = D // 2
HEADS = 6
HEAD_DIM = 64
WIDTH = HEADS * HEAD_DIM
PIX = 256
TOK = 8
SLOTS = 16
SIDE = 8
IMAGES = SIDE * SIDE
RING = 4
GROUP = 16
ROWS = GROUP * TOK
BF16 = jnp.bfloat16
F32 = jnp.float32

SHARD = (96, 96, 48, 96)
SPLIT = (48, 48, 32, 48)


def dot(a, b):
    return jnp.dot(a, b, preferred_element_type=F32)


def dot_nt(a, b):
    return lax.dot_general(a, b, (((1,), (1,)), ((), ())), preferred_element_type=F32)


def iota(shape, dim):
    return lax.broadcasted_iota(jnp.int32, shape, dim)


def kernel(
    tok_ref, pair_ref, count_ref, pose_ref, gq_ref, gk_ref, wkv_in, wq_in, wo_in, wh_in,
    joined_ref, grad_ref,
    wkv, wq, wo, wh, nkg, info_in, info, y_s, c_s, z_s, coef_s, hg, hin, tin,
    w_send, w_recv, n_send, n_recv, i_send, i_recv, g_send, g_recv, own_sem,
):
    scene, img = lax.axis_index("scene"), lax.axis_index("img")
    x, core = scene // 2, scene % 2
    yy, zz = img // SIDE, img % SIDE
    outer = (1 - core) * yy + core * zz
    inner = (1 - core) * zz + core * yy
    mypos = outer * SIDE + inner

    def img_of(o, n):
        return (1 - core) * (o * SIDE + n) + core * (n * SIDE + o)

    def turn(v, by):
        return lax.rem(v + by, SIDE)

    right = (lax.rem(x + 1, RING) * 2 + core, img)
    left = (lax.rem(x + 3, RING) * 2 + core, img)
    twin = (x * 2 + 1 - core, img)
    in_peer = [None] + [(scene, img_of(outer, turn(inner, k))) for k in range(1, SIDE)]
    out_peer = [None] + [(scene, img_of(turn(outer, k), inner)) for k in range(1, SIDE)]

    barrier = pltpu.get_barrier_semaphore()
    peers = [right, left, twin] + in_peer[1:] + out_peer[1:]
    for peer in peers:
        pl.semaphore_signal(barrier, inc=1, device_id=peer, device_id_type=pl.DeviceIdType.MESH)

    def remote(src, dst, send, recv, peer):
        return pltpu.make_async_remote_copy(
            src_ref=src, dst_ref=dst, send_sem=send, recv_sem=recv,
            device_id=peer, device_id_type=pl.DeviceIdType.MESH,
        )

    xt = tok_ref[0, 0].astype(F32)
    centered = xt - jnp.mean(xt, axis=-1, keepdims=True)
    normed = centered * lax.rsqrt(jnp.mean(centered * centered, axis=-1, keepdims=True) + 1e-05)
    nq = (normed * gq_ref[...].reshape(1, D)).astype(BF16)
    nk = normed * gk_ref[...].reshape(1, D)
    nkg[mypos] = jnp.concatenate([nk[:, :HALF], nk[:, HALF:]], axis=0).astype(BF16)

    lane = iota((1, 128), 1)
    count = count_ref[0, 0]
    row = jnp.full((1, 128), -1.0, F32)
    for k in range(SLOTS):
        first = pair_ref[0, 0, k, 0].astype(F32)
        second = pair_ref[0, 0, k, 1].astype(F32)
        live = (lane < 64) & (k >= count)
        hit = (lane == k) | (lane == 80 + k)
        row = jnp.where(hit & ~live, first, row)
        hit = (lane == 16 + k) | (lane == 64 + k)
        row = jnp.where(hit & ~live, second, row)
    tile = jnp.where(iota((SIDE, 128), 0) == inner, jnp.broadcast_to(row, (SIDE, 128)), 0.0)
    info_in[inner] = tile

    pl.semaphore_wait(barrier, len(peers))

    started = []
    for k in range(1, SIDE):
        copy = remote(nkg.at[mypos], nkg.at[mypos], n_send.at[0, k], n_recv.at[0, k], in_peer[k])
        copy.start()
        started.append(copy)
        copy = remote(info_in.at[inner], info_in.at[inner], i_send.at[0, k], i_recv.at[0, k], in_peer[k])
        copy.start()
        started.append(copy)

    sources = (wkv_in, wq_in, wo_in, wh_in)
    gathered = (wkv, wq, wo, wh)

    def part(a, s, lo=0, size=None):
        size = SHARD[a] if size is None else size
        return gathered[a].at[pl.ds(pl.multiple_of(s * SHARD[a] + lo, 16), size)]

    def shard_of(dx, dc):
        return lax.rem(x + dx + RING, RING) * 2 + (1 - core if dc else core)

    local = []
    for a in range(4):
        for n, peer in enumerate((right, left, twin)):
            copy = remote(sources[a], part(a, scene), w_send.at[a, n], w_recv.at[a, n], peer)
            copy.start()
            started.append(copy)
        copy = pltpu.make_async_copy(sources[a], part(a, scene), own_sem.at[a])
        copy.start()
        local.append(copy)

    for k in range(1, SIDE):
        src = outer * SIDE + turn(inner, SIDE - k)
        remote(nkg.at[src], nkg.at[src], n_send.at[0, k], n_recv.at[0, k], in_peer[k]).wait_recv()
        slot = turn(inner, SIDE - k)
        remote(info_in.at[slot], info_in.at[slot], i_send.at[0, k], i_recv.at[0, k], in_peer[k]).wait_recv()
    total = info_in[0]
    for k in range(1, SIDE):
        total = total + info_in[k]
    info[outer] = total
    block = nkg.at[pl.ds(outer * SIDE, SIDE)]
    for k in range(1, SIDE):
        copy = remote(block, block, n_send.at[1, k], n_recv.at[1, k], out_peer[k])
        copy.start()
        started.append(copy)
        copy = remote(info.at[outer], info.at[outer], i_send.at[1, k], i_recv.at[1, k], out_peer[k])
        copy.start()
        started.append(copy)

    def got(a, n, ref):
        remote(ref, ref, w_send.at[a, n], w_recv.at[a, n], twin).wait_recv()

    def send(a, n, ref, peer):
        copy = remote(ref, ref, w_send.at[a, n], w_recv.at[a, n], peer)
        copy.start()
        started.append(copy)

    for a in range(4):
        near = part(a, shard_of(-1, 0))
        got(a, 0, near)
        send(a, 3, part(a, shard_of(-1, 0), 0, SPLIT[a]), right)
        send(a, 5, near, twin)
        near = part(a, shard_of(1, 0))
        got(a, 1, near)
        send(a, 4, part(a, shard_of(1, 0), SPLIT[a], SHARD[a] - SPLIT[a]), left)
        send(a, 6, near, twin)
    for a in range(4):
        far = part(a, shard_of(2, 0), 0, SPLIT[a])
        got(a, 3, far)
        send(a, 7, far, twin)
        far = part(a, shard_of(2, 0), SPLIT[a], SHARD[a] - SPLIT[a])
        got(a, 4, far)
        send(a, 8, far, twin)

    for k in range(1, SIDE):
        slot = turn(outer, SIDE - k)
        remote(info.at[slot], info.at[slot], i_send.at[1, k], i_recv.at[1, k], out_peer[k]).wait_recv()
    table = info[...].reshape(IMAGES, 128)
    partner = pltpu.roll(table, 64, 1) + 1.0
    lanes = iota((IMAGES, 128), 1)
    match = table == img.astype(F32)
    ones = jnp.ones((SIDE, 128), F32)
    as_first = dot_nt(ones, jnp.where(match & (lanes < 16), partner, 0.0))
    as_second = dot_nt(ones, jnp.where(match & (lanes >= 16) & (lanes < 32), partner, 0.0))
    pos_row = iota((IMAGES, IMAGES), 0)
    pos_col = iota((IMAGES, IMAGES), 1)
    image_at = (1 - core) * pos_row + core * (pos_row % SIDE * SIDE + pos_row // SIDE)
    name = (image_at + 1).astype(F32)
    m1 = jnp.sum(jnp.where(as_first[0:1] == name, 1.0, 0.0), axis=1, keepdims=True)
    m2 = jnp.sum(jnp.where(as_second[0:1] == name, 1.0, 0.0), axis=1, keepdims=True)
    pose = jnp.concatenate([pose_ref[0], jnp.ones((IMAGES, 1), F32), jnp.zeros((IMAGES, 115), F32)], axis=1)
    pose = pose + jnp.where((lanes == 0) | (lanes == 4) | (lanes == 8), 1.0, 0.0)
    pose = jnp.dot(
        jnp.where(image_at == pos_col, 1.0, 0.0), pose,
        precision=lax.Precision.HIGHEST, preferred_element_type=F32,
    )
    mine = jnp.sum(jnp.where(iota((IMAGES, 128), 0) == mypos, pose, 0.0), axis=0, keepdims=True)
    coef = m1 * mine + m2 * pose
    coef_s[...] = jnp.broadcast_to(coef[:, None, :], (IMAGES, TOK, 128)).reshape(IMAGES * TOK, 128)

    for k in range(1, SIDE):
        src = nkg.at[pl.ds(turn(outer, SIDE - k) * SIDE, SIDE)]
        remote(src, src, n_send.at[1, k], n_recv.at[1, k], out_peer[k]).wait_recv()

    def finish(a):
        local[a].wait()
        got(a, 2, part(a, shard_of(0, 1)))
        got(a, 5, part(a, shard_of(-1, 1)))
        got(a, 6, part(a, shard_of(1, 1)))
        got(a, 7, part(a, shard_of(2, 1), 0, SPLIT[a]))
        got(a, 8, part(a, shard_of(2, 1), SPLIT[a], SHARD[a] - SPLIT[a]))

    finish(0)
    finish(1)
    q = dot(nq, wq[...]).astype(BF16).astype(F32) * HEAD_DIM ** (-0.5)
    qbig = jnp.concatenate([q] * HEADS, axis=0)
    own_head = iota((HEADS * TOK, WIDTH), 0) // TOK == iota((HEADS * TOK, WIDTH), 1) // HEAD_DIM
    qbig = jnp.where(own_head, qbig, 0.0).astype(BF16)
    finish(2)
    same = iota((ROWS, ROWS), 0) // TOK == iota((ROWS, ROWS), 1) // TOK
    head_of = iota((ROWS, WIDTH), 1) // HEAD_DIM
    x_tile = jnp.concatenate([xt] * GROUP, axis=0)

    def attend(g, carry):
        block = nkg[pl.ds(g * GROUP, GROUP)].astype(F32)
        low = block[:, :TOK].reshape(ROWS, HALF).astype(BF16)
        high = block[:, TOK:].reshape(ROWS, HALF).astype(BF16)
        kv = dot(low, wkv[:HALF]) + dot(high, wkv[HALF:])
        keys = kv[:, :WIDTH].astype(BF16)
        values = kv[:, WIDTH:].astype(BF16).astype(F32)
        scores = dot_nt(keys, qbig).reshape(GROUP, TOK, HEADS * TOK)
        e = jnp.exp(scores - jnp.max(scores, axis=1, keepdims=True))
        attn = (e / jnp.sum(e, axis=1, keepdims=True)).reshape(ROWS, HEADS * TOK)
        turned = attn.T
        spread = []
        for h in range(HEADS):
            piece = jnp.concatenate([turned[h * TOK:(h + 1) * TOK]] * GROUP, axis=0)
            spread.append(jnp.where(same, piece, 0.0).astype(BF16))
        split = [jnp.where(head_of == h, values, 0.0).astype(BF16) for h in range(HEADS)]
        o = dot(jnp.concatenate(spread, axis=1), jnp.concatenate(split, axis=0)).astype(BF16)
        y_s[pl.ds(pl.multiple_of(g * ROWS, ROWS), ROWS)] = (x_tile + dot(o, wo[...])).astype(BF16)
        return carry

    lax.fori_loop(0, IMAGES // GROUP, attend, 0)
    finish(3)

    def points(g, carry):
        rows = pl.ds(pl.multiple_of(g * ROWS, ROWS), ROWS)
        r = dot(y_s[rows], wh[...])
        cf = coef_s[rows]
        conf = 1.0 + jnp.exp(jnp.where(cf[:, 12:13] > 0.0, r[:, 3 * PIX:], 0.0))
        pts = [conf * r[:, k * PIX:(k + 1) * PIX] for k in range(3)]
        c_s[rows] = conf
        for n, value in enumerate(pts + [conf]):
            z_s[n, rows] = value[:, :128] + value[:, 128:]
        new = []
        for k in range(3):
            w = cf[:, 9 + k:10 + k] * conf
            for m in range(3):
                w = w + cf[:, 3 * k + m:3 * k + m + 1] * pts[m]
            new.append(carry[k] + jnp.sum(w.reshape(GROUP, TOK, PIX), axis=0))
        w = cf[:, 12:13] * conf
        new.append(carry[3] + jnp.sum(w.reshape(GROUP, TOK, PIX), axis=0))
        return tuple(new)

    zero = jnp.zeros((TOK, PIX), F32)
    sums = lax.fori_loop(0, IMAGES // GROUP, points, (zero,) * 4)
    joined = [(sums[k] / sums[3]).astype(BF16).astype(F32) for k in range(3)]
    joined_rows = [jnp.concatenate([j[t:t + 1] for t in range(TOK)], axis=1) for j in joined]
    joined_ref[0, 0] = jnp.concatenate(joined_rows, axis=0).astype(BF16)

    conf = c_s[...]
    coarse = conf.astype(BF16)
    fine = (conf - coarse.astype(F32)).astype(BF16)
    target = jnp.concatenate(joined, axis=0).astype(BF16)
    cross = dot_nt(coarse, target) + dot_nt(fine, target)
    agree = iota((IMAGES * TOK, 3 * TOK), 0) % TOK == iota((IMAGES * TOK, 3 * TOK), 1) % TOK
    cross = jnp.sum(jnp.where(agree, cross, 0.0).reshape(IMAGES, TOK, 3 * TOK), axis=1)
    channel = iota((IMAGES, 3 * TOK), 1) // TOK
    met = [jnp.sum(jnp.where(channel == k, cross, 0.0), axis=1, keepdims=True) for k in range(3)]
    total = [
        jnp.sum(jnp.sum(z_s[n].reshape(IMAGES, TOK, 128), axis=1), axis=1, keepdims=True)
        for n in range(4)
    ]
    sent = jnp.zeros((IMAGES, 128), F32)
    kept = jnp.zeros((1, 128), F32)
    for k in range(3):
        theirs = pose[:, 9 + k:10 + k] * total[3] - met[k]
        ours = mine[:, 9 + k:10 + k] * total[3] - met[k]
        for m in range(3):
            theirs = theirs + pose[:, 3 * k + m:3 * k + m + 1] * total[m]
            ours = ours + mine[:, 3 * k + m:3 * k + m + 1] * total[m]
        sent = jnp.where(lanes == k, m2 * theirs, sent)
        kept = jnp.where(lane == k, jnp.sum(m1 * ours, axis=0, keepdims=True), kept)
    hg[...] = sent.reshape(SIDE, SIDE, 128)

    for k in range(1, SIDE):
        to = turn(outer, k)
        copy = remote(hg.at[to], hin.at[outer], g_send.at[0, k], g_recv.at[0, k], out_peer[k])
        copy.start()
        started.append(copy)
    hin[outer] = hg[outer]
    for k in range(1, SIDE):
        slot = hin.at[turn(outer, SIDE - k)]
        remote(slot, slot, g_send.at[0, k], g_recv.at[0, k], out_peer[k]).wait_recv()
    tin[inner] = jnp.sum(hin[...], axis=0)
    for k in range(1, SIDE):
        slot = tin.at[inner]
        copy = remote(slot, slot, g_send.at[1, k], g_recv.at[1, k], in_peer[k])
        copy.start()
        started.append(copy)
    for k in range(1, SIDE):
        slot = tin.at[turn(inner, SIDE - k)]
        remote(slot, slot, g_send.at[1, k], g_recv.at[1, k], in_peer[k]).wait_recv()
    tiles = jnp.sum(tin[...], axis=0)
    row = jnp.sum(jnp.where(iota((SIDE, 128), 0) == inner, tiles, 0.0), axis=0, keepdims=True)
    grad_ref[0] = ((row + kept) * (2.0 / (TOK * PIX)))[:, :3]

    for copy in started:
        copy.wait_send()


def on_device(
    tokens, pair_list, pair_count, poses, gain_query, gain_kv, w_query, w_kv, w_out, w_head
):
    vmem = pl.BlockSpec(memory_space=pltpu.VMEM)
    smem = pl.BlockSpec(memory_space=pltpu.SMEM)
    hbm = pl.BlockSpec(memory_space=pl.ANY)
    dma = pltpu.SemaphoreType.DMA
    return pl.pallas_call(
        kernel,
        out_shape=(
            jax.ShapeDtypeStruct((1, 1, 3, TOK * PIX), BF16),
            jax.ShapeDtypeStruct((1, 1, 3), F32),
        ),
        in_specs=[vmem, smem, smem, vmem, vmem, vmem, hbm, hbm, hbm, hbm],
        out_specs=(vmem, vmem),
        scratch_shapes=[
            pltpu.VMEM((D, D), BF16),
            pltpu.VMEM((D, WIDTH), BF16),
            pltpu.VMEM((WIDTH, D), BF16),
            pltpu.VMEM((D, 4 * PIX), BF16),
            pltpu.VMEM((IMAGES, 2 * TOK, HALF), BF16),
            pltpu.VMEM((SIDE, SIDE, 128), F32),
            pltpu.VMEM((SIDE, SIDE, 128), F32),
            pltpu.VMEM((IMAGES * TOK, D), BF16),
            pltpu.VMEM((IMAGES * TOK, PIX), F32),
            pltpu.VMEM((4, IMAGES * TOK, 128), F32),
            pltpu.VMEM((IMAGES * TOK, 128), F32),
            pltpu.VMEM((SIDE, SIDE, 128), F32),
            pltpu.VMEM((SIDE, SIDE, 128), F32),
            pltpu.VMEM((SIDE, SIDE, 128), F32),
            dma((4, 9)),
            dma((4, 9)),
            dma((2, SIDE)),
            dma((2, SIDE)),
            dma((2, SIDE)),
            dma((2, SIDE)),
            dma((2, SIDE)),
            dma((2, SIDE)),
            dma((4,)),
        ],
        compiler_params=pltpu.CompilerParams(
            collective_id=0, has_side_effects=True, vmem_limit_bytes=40 * 1024 * 1024
        ),
    )(tokens, pair_list, pair_count, poses, gain_query, gain_kv, w_kv, w_query, w_out, w_head)


def solution(mesh):
    return jax.shard_map(
        on_device,
        mesh=mesh,
        in_specs=(
            P("scene", "img", None, None),
            P("scene", "img", None, None),
            P("scene", "img"),
            P("scene", None, None),
            P(),
            P(),
            P("scene", None),
            P("scene", None),
            P("scene", None),
            P("scene", None),
        ),
        out_specs=(P("scene", "img", None, None), P("scene", "img", None)),
        check_vma=False,
    )
```

```python
import jax
import jax.numpy as jnp
from jax import lax
from jax.experimental import pallas as pl
from jax.experimental.pallas import tpu as pltpu
from jax.sharding import PartitionSpec as P

D = 768
HALF = D // 2
HEADS = 6
HEAD_DIM = 64
WIDTH = HEADS * HEAD_DIM
PIX = 256
TOK = 8
SLOTS = 16
SIDE = 8
IMAGES = SIDE * SIDE
RING = 4
GROUP = 16
ROWS = GROUP * TOK
BF16 = jnp.bfloat16
F32 = jnp.float32

PIECES = ((0, 0, 96, 48), (1, 0, 96, 48), (2, 0, 48, 32), (2, 48, 48, 16), (3, 0, 48, 32))
SHARD = (96, 96, 96, 48)
NEAR_FIRST = (1, 7, 2, 6, 3, 5, 4)


def dot(a, b):
    return jnp.dot(a, b, preferred_element_type=F32)


def dot_nt(a, b):
    return lax.dot_general(a, b, (((1,), (1,)), ((), ())), preferred_element_type=F32)


def iota(shape, dim):
    return lax.broadcasted_iota(jnp.int32, shape, dim)


def kernel(
    tok_in, pair_in, count_in, pose_in, gq_in, gk_in, wkv_in, wq_in, wo_in, wh_in,
    joined_ref, grad_ref,
    tok_s, pair_s, count_s, pose_s, gq_s, gk_s, wkv, wq, wo, wh, nkg, info_in, info, kv_s, o_s, c_s, z_s, coef_s, hg, hin,
    w_send, w_recv, n_send, n_recv, i_send, i_recv, g_send, g_recv, own_sem, in_sem,
):
    scene, img = lax.axis_index("scene"), lax.axis_index("img")
    x, core = scene // 2, scene % 2
    yy, zz = img // SIDE, img % SIDE
    outer = (1 - core) * yy + core * zz
    inner = (1 - core) * zz + core * yy
    mypos = outer * SIDE + inner

    def img_of(o, n):
        return (1 - core) * (o * SIDE + n) + core * (n * SIDE + o)

    def turn(v, by):
        return lax.rem(v + by, SIDE)

    right = (lax.rem(x + 1, RING) * 2 + core, img)
    left = (lax.rem(x + 3, RING) * 2 + core, img)
    twin = (x * 2 + 1 - core, img)
    in_peer = [None] + [(scene, img_of(outer, turn(inner, k))) for k in range(1, SIDE)]
    out_peer = [None] + [(scene, img_of(turn(outer, k), inner)) for k in range(1, SIDE)]

    loads = []
    small = ((tok_in, tok_s), (gq_in, gq_s), (gk_in, gk_s), (pair_in, pair_s), (count_in, count_s), (pose_in, pose_s))
    for n, (src, dst) in enumerate(small):
        copy = pltpu.make_async_copy(src, dst, in_sem.at[n])
        copy.start()
        loads.append(copy)
    barrier = pltpu.get_barrier_semaphore()
    peers = [right, left, twin] + in_peer[1:] + out_peer[1:]
    for peer in peers:
        pl.semaphore_signal(barrier, inc=1, device_id=peer, device_id_type=pl.DeviceIdType.MESH)

    def remote(src, dst, send, recv, peer):
        return pltpu.make_async_remote_copy(
            src_ref=src, dst_ref=dst, send_sem=send, recv_sem=recv,
            device_id=peer, device_id_type=pl.DeviceIdType.MESH,
        )

    for copy in loads:
        copy.wait()
    xt = tok_s[0, 0].astype(F32)
    centered = xt - jnp.mean(xt, axis=-1, keepdims=True)
    normed = centered * lax.rsqrt(jnp.mean(centered * centered, axis=-1, keepdims=True) + 1e-05)
    nq = (normed * gq_s[...].reshape(1, D)).astype(BF16)
    nk = normed * gk_s[...].reshape(1, D)
    nkg[mypos] = jnp.concatenate([nk[:, :HALF], nk[:, HALF:]], axis=0).astype(BF16)

    lane = iota((1, 128), 1)
    first, second = pair_s[0, 0, 0:1].astype(F32), pair_s[0, 0, 1:2].astype(F32)
    live = iota((1, SLOTS), 1) < count_s[...]
    gap = jnp.full((1, 32), -1.0, F32)
    row = jnp.concatenate(
        [jnp.where(live, first, -1.0), jnp.where(live, second, -1.0), gap, second, first, gap], axis=1
    )
    tile = jnp.where(iota((SIDE, 128), 0) == inner, jnp.broadcast_to(row, (SIDE, 128)), 0.0)
    info_in[inner] = tile

    pl.semaphore_wait(barrier, len(peers))

    sources = (wkv_in, wq_in, wh_in, wo_in)
    gathered = (wkv, wq, wh, wo)

    def part(p, s, lo=0, size=None):
        a, first_row, rows, _ = PIECES[p]
        size = rows if size is None else size
        return gathered[a].at[pl.ds(pl.multiple_of(s * SHARD[a] + (first_row + lo), 16), size)]

    def shard_of(dx, dc):
        return lax.rem(x + dx + RING, RING) * 2 + (1 - core if dc else core)

    local = []

    def own(p):
        a, first_row, rows, _ = PIECES[p]
        src = sources[a].at[pl.ds(first_row, rows)]
        for n, peer in enumerate((right, left, twin)):
            copy = remote(src, part(p, scene), w_send.at[p, n], w_recv.at[p, n], peer)
            copy.start()
            started.append(copy)
        copy = pltpu.make_async_copy(src, part(p, scene), own_sem.at[p])
        copy.start()
        local.append(copy)

    def got(p, n, ref):
        remote(ref, ref, w_send.at[p, n], w_recv.at[p, n], twin).wait_recv()

    def send(p, n, ref, peer):
        copy = remote(ref, ref, w_send.at[p, n], w_recv.at[p, n], peer)
        copy.start()
        started.append(copy)

    def near(p):
        turn_at = PIECES[p][3]
        block = part(p, shard_of(-1, 0))
        got(p, 0, block)
        send(p, 3, part(p, shard_of(-1, 0), 0, turn_at), right)
        send(p, 5, block, twin)
        block = part(p, shard_of(1, 0))
        got(p, 1, block)
        send(p, 4, part(p, shard_of(1, 0), turn_at, PIECES[p][2] - turn_at), left)
        send(p, 6, block, twin)

    def far(p):
        turn_at = PIECES[p][3]
        block = part(p, shard_of(2, 0), 0, turn_at)
        got(p, 3, block)
        send(p, 7, block, twin)
        block = part(p, shard_of(2, 0), turn_at, PIECES[p][2] - turn_at)
        got(p, 4, block)
        send(p, 8, block, twin)

    def finish(p):
        turn_at = PIECES[p][3]
        local[p].wait()
        got(p, 2, part(p, shard_of(0, 1)))
        got(p, 5, part(p, shard_of(-1, 1)))
        got(p, 6, part(p, shard_of(1, 1)))
        got(p, 7, part(p, shard_of(2, 1), 0, turn_at))
        got(p, 8, part(p, shard_of(2, 1), turn_at, PIECES[p][2] - turn_at))

    started = []

    def tokens_out(ref, k):
        copy = remote(ref, ref, n_send.at[1, k], n_recv.at[1, k], out_peer[k])
        copy.start()

    own(0)
    mine_ref = nkg.at[mypos]
    for k in reversed(NEAR_FIRST):
        copy = remote(mine_ref, mine_ref, n_send.at[0, k], n_recv.at[0, k], in_peer[k])
        copy.start()
        started.append(copy)
    for k in reversed(NEAR_FIRST):
        slot = info_in.at[inner]
        copy = remote(slot, slot, i_send.at[0, k], i_recv.at[0, k], in_peer[k])
        copy.start()
        started.append(copy)
    for k in reversed(NEAR_FIRST):
        tokens_out(mine_ref, k)
    own(1)
    own(2)
    for k in NEAR_FIRST:
        arrived = nkg.at[outer * SIDE + turn(inner, SIDE - k)]
        remote(arrived, arrived, n_send.at[0, k], n_recv.at[0, k], in_peer[k]).wait_recv()
        for m in reversed(NEAR_FIRST):
            tokens_out(arrived, m)
    for k in NEAR_FIRST:
        slot = info_in.at[turn(inner, SIDE - k)]
        remote(slot, slot, i_send.at[0, k], i_recv.at[0, k], in_peer[k]).wait_recv()
    total = info_in[0]
    for k in range(1, SIDE):
        total = total + info_in[k]
    info[outer] = total
    for k in reversed(NEAR_FIRST):
        copy = remote(info.at[outer], info.at[outer], i_send.at[1, k], i_recv.at[1, k], out_peer[k])
        copy.start()
        started.append(copy)
    near(0)
    own(3)
    own(4)
    near(1)
    near(2)
    far(0)

    for k in range(1, SIDE):
        slot = turn(outer, SIDE - k)
        remote(info.at[slot], info.at[slot], i_send.at[1, k], i_recv.at[1, k], out_peer[k]).wait_recv()
    table = info[...].reshape(IMAGES, 128)
    partner = pltpu.roll(table, 64, 1) + 1.0
    lanes = iota((IMAGES, 128), 1)
    match = table == img.astype(F32)
    ones = jnp.ones((SIDE, 128), F32)
    as_first = dot_nt(ones, jnp.where(match & (lanes < 16), partner, 0.0))
    as_second = dot_nt(ones, jnp.where(match & (lanes >= 16) & (lanes < 32), partner, 0.0))
    pos_row = iota((IMAGES, IMAGES), 0)
    pos_col = iota((IMAGES, IMAGES), 1)
    image_at = (1 - core) * pos_row + core * (pos_row % SIDE * SIDE + pos_row // SIDE)
    name = (image_at + 1).astype(F32)
    m1 = jnp.sum(jnp.where(as_first[0:1] == name, 1.0, 0.0), axis=1, keepdims=True)
    m2 = jnp.sum(jnp.where(as_second[0:1] == name, 1.0, 0.0), axis=1, keepdims=True)
    pose = jnp.concatenate(
        [pose_s[:, 0], jnp.ones((1, IMAGES), F32), jnp.zeros((115, IMAGES), F32)], axis=0
    )
    number = iota((128, IMAGES), 0)
    pose = pose + jnp.where((number == 0) | (number == 4) | (number == 8), 1.0, 0.0)
    pose = lax.dot_general(
        jnp.where(image_at == pos_col, 1.0, 0.0), pose, (((1,), (1,)), ((), ())),
        precision=lax.Precision.HIGHEST, preferred_element_type=F32,
    )
    mine = jnp.sum(jnp.where(iota((IMAGES, 128), 0) == mypos, pose, 0.0), axis=0, keepdims=True)
    coef = m1 * mine + m2 * pose
    coef_s[...] = jnp.broadcast_to(coef[:, None, :], (IMAGES, TOK, 128)).reshape(IMAGES * TOK, 128)

    for k in range(1, SIDE):
        src = nkg.at[pl.ds(turn(outer, SIDE - k) * SIDE, SIDE)]
        remote(src, src, n_send.at[1, k], n_recv.at[1, k], out_peer[k]).wait_recv()

    finish(0)

    def keys_values(g, carry):
        block = nkg[pl.ds(g * GROUP, GROUP)].astype(F32)
        low = block[:, :TOK].reshape(ROWS, HALF).astype(BF16)
        high = block[:, TOK:].reshape(ROWS, HALF).astype(BF16)
        rows = pl.ds(pl.multiple_of(g * ROWS, ROWS), ROWS)
        kv_s[rows] = (dot(low, wkv[:HALF]) + dot(high, wkv[HALF:])).astype(BF16)
        return carry

    lax.fori_loop(0, IMAGES // GROUP, keys_values, 0)
    near(3)
    near(4)
    far(1)
    finish(1)
    q = dot(nq, wq[...]).astype(BF16).astype(F32) * HEAD_DIM ** (-0.5)
    qbig = jnp.concatenate([q] * HEADS, axis=0)
    own_head = iota((HEADS * TOK, WIDTH), 0) // TOK == iota((HEADS * TOK, WIDTH), 1) // HEAD_DIM
    qbig = jnp.where(own_head, qbig, 0.0).astype(BF16)
    same = iota((ROWS, ROWS), 0) // TOK == iota((ROWS, ROWS), 1) // TOK
    head_of = iota((ROWS, WIDTH), 1) // HEAD_DIM
    x_tile = jnp.concatenate([xt] * GROUP, axis=0)

    def attend(g, carry):
        rows = pl.ds(pl.multiple_of(g * ROWS, ROWS), ROWS)
        keys = kv_s[rows, :WIDTH]
        values = kv_s[rows, WIDTH:].astype(F32)
        scores = dot_nt(keys, qbig).reshape(GROUP, TOK, HEADS * TOK)
        e = jnp.exp(scores - jnp.max(scores, axis=1, keepdims=True))
        attn = (e / jnp.sum(e, axis=1, keepdims=True)).reshape(ROWS, HEADS * TOK)
        turned = attn.T
        spread = []
        for h in range(HEADS):
            piece = jnp.concatenate([turned[h * TOK:(h + 1) * TOK]] * GROUP, axis=0)
            spread.append(jnp.where(same, piece, 0.0).astype(BF16))
        split = [jnp.where(head_of == h, values, 0.0).astype(BF16) for h in range(HEADS)]
        o = dot(jnp.concatenate(spread, axis=1), jnp.concatenate(split, axis=0))
        o_s[rows] = o.astype(BF16)
        return carry

    lax.fori_loop(0, 2, attend, 0)
    far(2)
    lax.fori_loop(2, IMAGES // GROUP, attend, 0)
    far(3)
    far(4)
    finish(2)
    finish(3)
    finish(4)

    def points(g, carry):
        rows = pl.ds(pl.multiple_of(g * ROWS, ROWS), ROWS)
        y = (x_tile + dot(o_s[rows], wo[...])).astype(BF16)
        r = dot(y, wh[...])
        cf = coef_s[rows]
        conf = 1.0 + jnp.exp(jnp.where(cf[:, 12:13] > 0.0, r[:, 3 * PIX:], 0.0))
        pts = [conf * r[:, k * PIX:(k + 1) * PIX] for k in range(3)]
        c_s[rows] = conf
        for n, value in enumerate(pts + [conf]):
            z_s[n, rows] = value[:, :128] + value[:, 128:]
        new = []
        for k in range(3):
            w = cf[:, 9 + k:10 + k] * conf
            for m in range(3):
                w = w + cf[:, 3 * k + m:3 * k + m + 1] * pts[m]
            new.append(carry[k] + jnp.sum(w.reshape(GROUP, TOK, PIX), axis=0))
        w = cf[:, 12:13] * conf
        new.append(carry[3] + jnp.sum(w.reshape(GROUP, TOK, PIX), axis=0))
        return tuple(new)

    zero = jnp.zeros((TOK, PIX), F32)
    sums = lax.fori_loop(0, IMAGES // GROUP, points, (zero,) * 4)
    joined = [(sums[k] / sums[3]).astype(BF16).astype(F32) for k in range(3)]
    joined_rows = [jnp.concatenate([j[t:t + 1] for t in range(TOK)], axis=1) for j in joined]
    joined_ref[0, 0] = jnp.concatenate(joined_rows, axis=0).astype(BF16)

    conf = c_s[...]
    coarse = conf.astype(BF16)
    fine = (conf - coarse.astype(F32)).astype(BF16)
    target = jnp.concatenate(joined, axis=0).astype(BF16)
    cross = dot_nt(coarse, target) + dot_nt(fine, target)
    agree = iota((IMAGES * TOK, 3 * TOK), 0) % TOK == iota((IMAGES * TOK, 3 * TOK), 1) % TOK
    cross = jnp.sum(jnp.where(agree, cross, 0.0).reshape(IMAGES, TOK, 3 * TOK), axis=1)
    channel = iota((IMAGES, 3 * TOK), 1) // TOK
    met = [jnp.sum(jnp.where(channel == k, cross, 0.0), axis=1, keepdims=True) for k in range(3)]
    total = [
        jnp.sum(jnp.sum(z_s[n].reshape(IMAGES, TOK, 128), axis=1), axis=1, keepdims=True)
        for n in range(4)
    ]
    sent = jnp.zeros((IMAGES, 128), F32)
    kept = jnp.zeros((1, 128), F32)
    for k in range(3):
        theirs = pose[:, 9 + k:10 + k] * total[3] - met[k]
        ours = mine[:, 9 + k:10 + k] * total[3] - met[k]
        for m in range(3):
            theirs = theirs + pose[:, 3 * k + m:3 * k + m + 1] * total[m]
            ours = ours + mine[:, 3 * k + m:3 * k + m + 1] * total[m]
        sent = jnp.where(lanes == k, m2 * theirs, sent)
        kept = jnp.where(lane == k, jnp.sum(m1 * ours, axis=0, keepdims=True), kept)
    hg[...] = sent.reshape(IMAGES, 1, 128)

    def give(n, carry):
        o, i = turn(outer, n // SIDE), turn(inner, n % SIDE)
        remote(hg.at[o * SIDE + i], hin.at[mypos], g_send.at[0], g_recv.at[0], (scene, img_of(o, i))).start()
        return carry

    lax.fori_loop(36, IMAGES, give, 0)
    lax.fori_loop(1, 36, give, 0)
    hin[mypos] = jnp.zeros((1, 128), F32)
    most = hin.at[pl.ds(0, IMAGES - 1)]
    exchange = remote(most, most, g_send.at[0], g_recv.at[0], twin)
    exchange.wait_recv()
    row = jnp.sum(hin[...], axis=0)
    grad_ref[0] = ((row + kept) * (2.0 / (TOK * PIX)))[:, :3]

    exchange.wait_send()
    all_tokens = nkg.at[pl.ds(outer * SIDE, SIDE)]
    for k in range(1, SIDE):
        remote(all_tokens, all_tokens, n_send.at[1, k], n_recv.at[1, k], out_peer[k]).wait_send()
    for copy in started:
        copy.wait_send()


def on_device(
    tokens, pair_list, pair_count, poses, gain_query, gain_kv, w_query, w_kv, w_out, w_head
):
    vmem = pl.BlockSpec(memory_space=pltpu.VMEM)
    hbm = pl.BlockSpec(memory_space=pltpu.HBM)
    dma = pltpu.SemaphoreType.DMA
    return pl.pallas_call(
        kernel,
        out_shape=(
            jax.ShapeDtypeStruct((1, 1, 3, TOK * PIX), BF16),
            jax.ShapeDtypeStruct((1, 1, 3), F32),
        ),
        in_specs=[hbm] * 10,
        out_specs=(vmem, vmem),
        scratch_shapes=[
            pltpu.VMEM((1, 1, TOK, D), BF16),
            pltpu.VMEM((1, 1, 2, SLOTS), jnp.int32),
            pltpu.VMEM((1, 1), jnp.int32),
            pltpu.VMEM((12, 1, IMAGES), F32),
            pltpu.VMEM((D,), F32),
            pltpu.VMEM((D,), F32),
            pltpu.VMEM((D, D), BF16),
            pltpu.VMEM((D, WIDTH), BF16),
            pltpu.VMEM((WIDTH, D), BF16),
            pltpu.VMEM((D, 4 * PIX), BF16),
            pltpu.VMEM((IMAGES, 2 * TOK, HALF), BF16),
            pltpu.VMEM((SIDE, SIDE, 128), F32),
            pltpu.VMEM((SIDE, SIDE, 128), F32),
            pltpu.VMEM((IMAGES * TOK, D), BF16),
            pltpu.VMEM((IMAGES * TOK, WIDTH), BF16),
            pltpu.VMEM((IMAGES * TOK, PIX), F32),
            pltpu.VMEM((4, IMAGES * TOK, 128), F32),
            pltpu.VMEM((IMAGES * TOK, 128), F32),
            pltpu.VMEM((IMAGES, 1, 128), F32),
            pltpu.VMEM((IMAGES, 1, 128), F32),
            dma((5, 9)),
            dma((5, 9)),
            dma((2, SIDE)),
            dma((2, SIDE)),
            dma((2, SIDE)),
            dma((2, SIDE)),
            dma((1,)),
            dma((1,)),
            dma((5,)),
            dma((6,)),
        ],
        compiler_params=pltpu.CompilerParams(
            collective_id=0, has_side_effects=True, vmem_limit_bytes=64 * 1024 * 1024
        ),
    )(
        tokens, jnp.swapaxes(pair_list, 2, 3), pair_count, jnp.transpose(poses, (2, 0, 1)),
        gain_query, gain_kv, w_kv, w_query, w_out, w_head,
    )


def solution(mesh):
    return jax.shard_map(
        on_device,
        mesh=mesh,
        in_specs=(
            P("scene", "img", None, None),
            P("scene", "img", None, None),
            P("scene", "img"),
            P("scene", None, None),
            P(),
            P(),
            P("scene", None),
            P("scene", None),
            P("scene", None),
            P("scene", None),
        ),
        out_specs=(P("scene", "img", None, None), P("scene", "img", None)),
        check_vma=False,
    )
```

```python
import jax
import jax.numpy as jnp
from jax import lax
from jax.experimental import pallas as pl
from jax.experimental.pallas import tpu as pltpu
from jax.sharding import PartitionSpec as P

D = 768
HALF = D // 2
HEADS = 6
HEAD_DIM = 64
WIDTH = HEADS * HEAD_DIM
PIX = 256
TOK = 8
SLOTS = 16
SIDE = 8
IMAGES = SIDE * SIDE
RING = 4
GROUP = 16
ROWS = GROUP * TOK
WIDE = 32
MANY = WIDE * TOK
BF16 = jnp.bfloat16
F32 = jnp.float32

SHARD = 96
MID = SHARD // 2
OUT = 4 * PIX
RING_ORDER = (0, 1, 7, 2, 6, 3, 5, 4)
NEAR_FIRST = RING_ORDER[1:]
EARLY = 3


def dot(a, b):
    return jnp.dot(a, b, preferred_element_type=F32)


def dot_nt(a, b):
    return lax.dot_general(a, b, (((1,), (1,)), ((), ())), preferred_element_type=F32)


def iota(shape, dim):
    return lax.broadcasted_iota(jnp.int32, shape, dim)


def kernel(
    tok_in, pair_in, count_in, pose_in, gq_in, gk_in, wkv_in, wq_in, wo_in, wh_in,
    joined_ref, grad_ref,
    tok_s, pair_s, count_s, pose_s, gq_s, gk_s, wa, wb, wo, nkg, info_in, info, o_s, c_s, z_s, coef_s, hg, hin,
    w_send, w_recv, n_send, n_recv, i_send, i_recv, g_send, g_recv, in_sem,
):
    scene, img = lax.axis_index("scene"), lax.axis_index("img")
    x, core = scene // 2, scene % 2
    yy, zz = img // SIDE, img % SIDE
    outer = (1 - core) * yy + core * zz
    inner = (1 - core) * zz + core * yy
    mypos = outer * SIDE
    myname = outer * SIDE + inner

    def img_of(o, n):
        return (1 - core) * (o * SIDE + n) + core * (n * SIDE + o)

    def turn(v, by):
        return lax.rem(v + by, SIDE)

    right = (lax.rem(x + 1, RING) * 2 + core, img)
    left = (lax.rem(x + 3, RING) * 2 + core, img)
    twin = (x * 2 + 1 - core, img)
    in_peer = [None] + [(scene, img_of(outer, turn(inner, k))) for k in range(1, SIDE)]
    out_peer = [None] + [(scene, img_of(turn(outer, k), inner)) for k in range(1, SIDE)]

    barrier = pltpu.get_barrier_semaphore()
    peers = [right, left, twin] + in_peer[1:] + out_peer[1:]
    for peer in peers:
        pl.semaphore_signal(barrier, inc=1, device_id=peer, device_id_type=pl.DeviceIdType.MESH)

    loads = []
    row0 = pl.ds(pl.multiple_of(scene * SHARD, SHARD), SHARD)
    top = pl.ds(pl.multiple_of(scene * SHARD, 16), MID)
    bottom = pl.ds(pl.multiple_of(scene * SHARD + MID, 16), MID)
    copies = (
        (tok_in, tok_s), (gq_in, gq_s), (gk_in, gk_s), (pair_in, pair_s), (count_in, count_s),
        (pose_in, pose_s),
        (wq_in, wa.at[row0, pl.ds(0, WIDTH)]), (wkv_in, wa.at[row0, pl.ds(WIDTH, D)]),
        (wh_in, wb.at[row0, pl.ds(0, OUT)]),
        (wo_in.at[:, pl.ds(0, HALF)], wb.at[top, pl.ds(OUT, HALF)]),
        (wo_in.at[:, pl.ds(HALF, HALF)], wb.at[bottom, pl.ds(OUT, HALF)]),
    )
    for n, (src, dst) in enumerate(copies):
        copy = pltpu.make_async_copy(src, dst, in_sem.at[n])
        copy.start()
        loads.append(copy)

    def remote(src, dst, send, recv, peer):
        return pltpu.make_async_remote_copy(
            src_ref=src, dst_ref=dst, send_sem=send, recv_sem=recv,
            device_id=peer, device_id_type=pl.DeviceIdType.MESH,
        )

    for copy in loads[:6]:
        copy.wait()
    xt = tok_s[0, 0].astype(F32)
    centered = xt - jnp.mean(xt, axis=-1, keepdims=True)
    normed = centered * lax.rsqrt(jnp.mean(centered * centered, axis=-1, keepdims=True) + 1e-05)
    nq = (normed * gq_s[...].reshape(1, D)).astype(BF16)
    nk = normed * gk_s[...].reshape(1, D)
    nkg[mypos] = jnp.concatenate([nk[:, :HALF], nk[:, HALF:]], axis=0).astype(BF16)

    lane = iota((1, 128), 1)
    first, second = pair_s[0, 0, 0:1].astype(F32), pair_s[0, 0, 1:2].astype(F32)
    live = iota((1, SLOTS), 1) < count_s[...]
    gap = jnp.full((1, 32), -1.0, F32)
    row = jnp.concatenate(
        [jnp.where(live, first, -1.0), jnp.where(live, second, -1.0), gap, second, first, gap], axis=1
    )
    tile = jnp.where(iota((SIDE, 128), 0) == inner, jnp.broadcast_to(row, (SIDE, 128)), 0.0)
    info_in[inner] = tile

    for copy in loads[6:]:
        copy.wait()
    pl.semaphore_wait(barrier, len(peers))

    gathered = (wa, wb)

    def part(p, s, lo=0, size=SHARD):
        return gathered[p].at[pl.ds(pl.multiple_of(s * SHARD + lo, 16), size)]

    def shard_of(dx, dc):
        return lax.rem(x + dx + RING, RING) * 2 + (1 - core if dc else core)

    started = []

    def send(p, n, ref, peer):
        copy = remote(ref, ref, w_send.at[p, n], w_recv.at[p, n], peer)
        copy.start()
        started.append(copy)

    def got(p, n, ref):
        remote(ref, ref, w_send.at[p, n], w_recv.at[p, n], twin).wait_recv()

    def own(p):
        for n, peer in enumerate((right, left, twin)):
            send(p, n, part(p, scene), peer)

    def near(p):
        got(p, 0, part(p, shard_of(-1, 0)))
        send(p, 3, part(p, shard_of(-1, 0), 0, MID), right)
        send(p, 5, part(p, shard_of(-1, 0)), twin)
        got(p, 1, part(p, shard_of(1, 0)))
        send(p, 4, part(p, shard_of(1, 0), MID, MID), left)
        send(p, 6, part(p, shard_of(1, 0)), twin)

    def far(p):
        got(p, 3, part(p, shard_of(2, 0), 0, MID))
        send(p, 7, part(p, shard_of(2, 0), 0, MID), twin)
        got(p, 4, part(p, shard_of(2, 0), MID, MID))
        send(p, 8, part(p, shard_of(2, 0), MID, MID), twin)

    def finish(p):
        got(p, 2, part(p, shard_of(0, 1)))
        got(p, 5, part(p, shard_of(-1, 1)))
        got(p, 6, part(p, shard_of(1, 1)))
        got(p, 7, part(p, shard_of(2, 1), 0, MID))
        got(p, 8, part(p, shard_of(2, 1), MID, MID))

    own(0)
    for k in reversed(NEAR_FIRST):
        slot = nkg.at[mypos + RING_ORDER.index(k)]
        copy = remote(nkg.at[mypos], slot, n_send.at[0, k], n_recv.at[0, k], in_peer[k])
        copy.start()
        started.append(copy)
    own(1)
    for k in reversed(NEAR_FIRST):
        slot = info_in.at[inner]
        copy = remote(slot, slot, i_send.at[0, k], i_recv.at[0, k], in_peer[k])
        copy.start()
        started.append(copy)

    def arrive(k):
        slot = nkg.at[mypos + RING_ORDER.index(k)]
        remote(slot, slot, n_send.at[0, k], n_recv.at[0, k], in_peer[k]).wait_recv()

    def pass_on(lo, size):
        group = nkg.at[pl.ds(mypos + lo, size)]
        for k in reversed(NEAR_FIRST):
            remote(group, group, n_send.at[1, k], n_recv.at[1, k], out_peer[k]).start()

    for k in RING_ORDER[1:EARLY]:
        arrive(k)
    pass_on(0, EARLY)
    for k in RING_ORDER[EARLY:]:
        arrive(k)
    for k in NEAR_FIRST:
        slot = info_in.at[turn(inner, SIDE - k)]
        remote(slot, slot, i_send.at[0, k], i_recv.at[0, k], in_peer[k]).wait_recv()
    total = info_in[0]
    for k in range(1, SIDE):
        total = total + info_in[k]
    info[outer] = total
    for k in reversed(NEAR_FIRST):
        copy = remote(info.at[outer], info.at[outer], i_send.at[1, k], i_recv.at[1, k], out_peer[k])
        copy.start()
        started.append(copy)
    pass_on(EARLY, SIDE - EARLY)
    near(0)
    near(1)
    far(0)

    for k in range(1, SIDE):
        slot = turn(outer, SIDE - k)
        remote(info.at[slot], info.at[slot], i_send.at[1, k], i_recv.at[1, k], out_peer[k]).wait_recv()
    table = info[...].reshape(IMAGES, 128)
    partner = pltpu.roll(table, 64, 1) + 1.0
    lanes = iota((IMAGES, 128), 1)
    match = table == img.astype(F32)
    ones = jnp.ones((SIDE, 128), F32)
    as_first = dot_nt(ones, jnp.where(match & (lanes < 16), partner, 0.0))
    as_second = dot_nt(ones, jnp.where(match & (lanes >= 16) & (lanes < 32), partner, 0.0))
    pos_row = iota((IMAGES, IMAGES), 0)
    pos_col = iota((IMAGES, IMAGES), 1)
    slot = pos_row % SIDE
    back = (slot % 2) * ((slot + 1) // 2) + (1 - slot % 2) * (SIDE - slot // 2)
    place = (inner - back + 2 * SIDE) % SIDE
    image_at = (1 - core) * (pos_row // SIDE * SIDE + place) + core * (place * SIDE + pos_row // SIDE)
    name = (image_at + 1).astype(F32)
    m1 = jnp.sum(jnp.where(as_first[0:1] == name, 1.0, 0.0), axis=1, keepdims=True)
    m2 = jnp.sum(jnp.where(as_second[0:1] == name, 1.0, 0.0), axis=1, keepdims=True)
    pose = jnp.concatenate(
        [pose_s[:, 0], jnp.ones((1, IMAGES), F32), jnp.zeros((115, IMAGES), F32)], axis=0
    )
    number = iota((128, IMAGES), 0)
    pose = pose + jnp.where((number == 0) | (number == 4) | (number == 8), 1.0, 0.0)
    pose = lax.dot_general(
        jnp.where(image_at == pos_col, 1.0, 0.0), pose, (((1,), (1,)), ((), ())),
        precision=lax.Precision.HIGHEST, preferred_element_type=F32,
    )
    mine = jnp.sum(jnp.where(iota((IMAGES, 128), 0) == mypos, pose, 0.0), axis=0, keepdims=True)
    coef = m1 * mine + m2 * pose
    coef_s[...] = jnp.broadcast_to(coef[:, None, :], (IMAGES, TOK, 128)).reshape(IMAGES * TOK, 128)

    for k in range(1, SIDE):
        src = nkg.at[pl.ds(turn(outer, SIDE - k) * SIDE, SIDE)]
        remote(src, src, n_send.at[1, k], n_recv.at[1, k], out_peer[k]).wait_recv()

    finish(0)
    q = dot(nq, wa[:, :WIDTH]).astype(BF16).astype(F32) * HEAD_DIM ** (-0.5)
    qbig = jnp.concatenate([q] * HEADS, axis=0)
    own_head = iota((HEADS * TOK, WIDTH), 0) // TOK == iota((HEADS * TOK, WIDTH), 1) // HEAD_DIM
    qbig = jnp.where(own_head, qbig, 0.0).astype(BF16)
    same = iota((ROWS, ROWS), 0) // TOK == iota((ROWS, ROWS), 1) // TOK
    head_of = iota((ROWS, WIDTH), 1) // HEAD_DIM
    x_tile = jnp.concatenate([xt] * WIDE, axis=0)

    def attend(g, carry):
        rows = pl.ds(pl.multiple_of(g * ROWS, ROWS), ROWS)
        block = nkg[pl.ds(g * GROUP, GROUP)].astype(F32)
        low = block[:, :TOK].reshape(ROWS, HALF).astype(BF16)
        high = block[:, TOK:].reshape(ROWS, HALF).astype(BF16)
        kv = dot(low, wa[:HALF, WIDTH:]) + dot(high, wa[HALF:, WIDTH:])
        keys = kv[:, :WIDTH].astype(BF16)
        values = kv[:, WIDTH:].astype(BF16).astype(F32)
        scores = dot_nt(keys, qbig).reshape(GROUP, TOK, HEADS * TOK)
        e = jnp.exp(scores - jnp.max(scores, axis=1, keepdims=True))
        attn = (e / jnp.sum(e, axis=1, keepdims=True)).reshape(ROWS, HEADS * TOK)
        turned = attn.T
        spread = []
        for h in range(HEADS):
            piece = jnp.concatenate([turned[h * TOK:(h + 1) * TOK]] * GROUP, axis=0)
            spread.append(jnp.where(same, piece, 0.0).astype(BF16))
        split = [jnp.where(head_of == h, values, 0.0).astype(BF16) for h in range(HEADS)]
        o = dot(jnp.concatenate(spread, axis=1), jnp.concatenate(split, axis=0))
        o_s[rows] = o.astype(BF16)
        return carry

    lax.fori_loop(0, 2, attend, 0)
    far(1)
    lax.fori_loop(2, IMAGES // GROUP, attend, 0)
    finish(1)
    for s in range(D // SHARD):
        wo[s * MID:(s + 1) * MID, :HALF] = wb[s * SHARD:s * SHARD + MID, OUT:]
        wo[s * MID:(s + 1) * MID, HALF:] = wb[s * SHARD + MID:(s + 1) * SHARD, OUT:]

    def points(g, carry):
        rows = pl.ds(pl.multiple_of(g * MANY, MANY), MANY)
        y = (x_tile + dot(o_s[rows], wo[...])).astype(BF16)
        r = dot(y, wb[:, :OUT])
        cf = coef_s[rows]
        conf = 1.0 + jnp.exp(jnp.where(cf[:, 12:13] > 0.0, r[:, 3 * PIX:], 0.0))
        pts = [conf * r[:, k * PIX:(k + 1) * PIX] for k in range(3)]
        c_s[rows] = conf
        for n, value in enumerate(pts + [conf]):
            z_s[n, rows] = value[:, :128] + value[:, 128:]
        new = []
        for k in range(3):
            w = cf[:, 9 + k:10 + k] * conf
            for m in range(3):
                w = w + cf[:, 3 * k + m:3 * k + m + 1] * pts[m]
            new.append(carry[k] + jnp.sum(w.reshape(WIDE, TOK, PIX), axis=0))
        w = cf[:, 12:13] * conf
        new.append(carry[3] + jnp.sum(w.reshape(WIDE, TOK, PIX), axis=0))
        return tuple(new)

    zero = jnp.zeros((TOK, PIX), F32)
    sums = lax.fori_loop(0, IMAGES // WIDE, points, (zero,) * 4)
    joined = [(sums[k] / sums[3]).astype(BF16).astype(F32) for k in range(3)]
    joined_rows = [jnp.concatenate([j[t:t + 1] for t in range(TOK)], axis=1) for j in joined]
    joined_ref[0, 0] = jnp.concatenate(joined_rows, axis=0).astype(BF16)

    conf = c_s[...]
    coarse = conf.astype(BF16)
    fine = (conf - coarse.astype(F32)).astype(BF16)
    target = jnp.concatenate(joined, axis=0).astype(BF16)
    cross = dot_nt(coarse, target) + dot_nt(fine, target)
    agree = iota((IMAGES * TOK, 3 * TOK), 0) % TOK == iota((IMAGES * TOK, 3 * TOK), 1) % TOK
    cross = jnp.sum(jnp.where(agree, cross, 0.0).reshape(IMAGES, TOK, 3 * TOK), axis=1)
    channel = iota((IMAGES, 3 * TOK), 1) // TOK
    met = [jnp.sum(jnp.where(channel == k, cross, 0.0), axis=1, keepdims=True) for k in range(3)]
    total = [
        jnp.sum(jnp.sum(z_s[n].reshape(IMAGES, TOK, 128), axis=1), axis=1, keepdims=True)
        for n in range(4)
    ]
    sent = jnp.zeros((IMAGES, 128), F32)
    kept = jnp.zeros((1, 128), F32)
    for k in range(3):
        theirs = pose[:, 9 + k:10 + k] * total[3] - met[k]
        ours = mine[:, 9 + k:10 + k] * total[3] - met[k]
        for m in range(3):
            theirs = theirs + pose[:, 3 * k + m:3 * k + m + 1] * total[m]
            ours = ours + mine[:, 3 * k + m:3 * k + m + 1] * total[m]
        sent = jnp.where(lanes == k, m2 * theirs, sent)
        kept = jnp.where(lane == k, jnp.sum(m1 * ours, axis=0, keepdims=True), kept)
    hg[...] = sent.reshape(IMAGES, 1, 128)

    def give(o, k):
        src = hg.at[o * SIDE + RING_ORDER.index((SIDE - k) % SIDE)]
        peer = (scene, img_of(o, turn(inner, k)))
        remote(src, hin.at[myname], g_send.at[0], g_recv.at[0], peer).start()

    def give_row(n, carry):
        u = SIDE - 1 - n
        o = turn(outer, (u % 2) * ((u + 1) // 2) + (1 - u % 2) * (SIDE - u // 2))
        for k in reversed(RING_ORDER):
            give(o, k)
        return carry

    lax.fori_loop(0, SIDE - 1, give_row, 0)
    for k in reversed(NEAR_FIRST):
        give(outer, k)
    hin[myname] = jnp.zeros((1, 128), F32)
    for copy in started:
        copy.wait_send()
    all_tokens = nkg.at[pl.ds(mypos, SIDE)]
    for k in range(1, SIDE):
        remote(all_tokens, all_tokens, n_send.at[1, k], n_recv.at[1, k], out_peer[k]).wait_send()
    most = hin.at[pl.ds(0, IMAGES - 1)]
    exchange = remote(most, most, g_send.at[0], g_recv.at[0], twin)
    exchange.wait_send()
    exchange.wait_recv()
    row = jnp.sum(hin[...], axis=0)
    grad_ref[0] = ((row + kept) * (2.0 / (TOK * PIX)))[:, :3]


def on_device(
    tokens, pair_list, pair_count, poses, gain_query, gain_kv, w_query, w_kv, w_out, w_head
):
    vmem = pl.BlockSpec(memory_space=pltpu.VMEM)
    hbm = pl.BlockSpec(memory_space=pltpu.HBM)
    dma = pltpu.SemaphoreType.DMA
    return pl.pallas_call(
        kernel,
        out_shape=(
            jax.ShapeDtypeStruct((1, 1, 3, TOK * PIX), BF16),
            jax.ShapeDtypeStruct((1, 1, 3), F32),
        ),
        in_specs=[hbm] * 10,
        out_specs=(vmem, vmem),
        scratch_shapes=[
            pltpu.VMEM((1, 1, TOK, D), BF16),
            pltpu.VMEM((1, 1, 2, SLOTS), jnp.int32),
            pltpu.VMEM((1, 1), jnp.int32),
            pltpu.VMEM((12, 1, IMAGES), F32),
            pltpu.VMEM((D,), F32),
            pltpu.VMEM((D,), F32),
            pltpu.VMEM((D, WIDTH + D), BF16),
            pltpu.VMEM((D, OUT + HALF), BF16),
            pltpu.VMEM((WIDTH, D), BF16),
            pltpu.VMEM((IMAGES, 2 * TOK, HALF), BF16),
            pltpu.VMEM((SIDE, SIDE, 128), F32),
            pltpu.VMEM((SIDE, SIDE, 128), F32),
            pltpu.VMEM((IMAGES * TOK, WIDTH), BF16),
            pltpu.VMEM((IMAGES * TOK, PIX), F32),
            pltpu.VMEM((4, IMAGES * TOK, 128), F32),
            pltpu.VMEM((IMAGES * TOK, 128), F32),
            pltpu.VMEM((IMAGES, 1, 128), F32),
            pltpu.VMEM((IMAGES, 1, 128), F32),
            dma((2, 9)),
            dma((2, 9)),
            dma((2, SIDE)),
            dma((2, SIDE)),
            dma((2, SIDE)),
            dma((2, SIDE)),
            dma((1,)),
            dma((1,)),
            dma((11,)),
        ],
        compiler_params=pltpu.CompilerParams(
            collective_id=0, has_side_effects=True, vmem_limit_bytes=64 * 1024 * 1024
        ),
    )(
        tokens, jnp.swapaxes(pair_list, 2, 3), pair_count, jnp.transpose(poses, (2, 0, 1)),
        gain_query, gain_kv, w_kv, w_query, w_out, w_head,
    )


def solution(mesh):
    return jax.shard_map(
        on_device,
        mesh=mesh,
        in_specs=(
            P("scene", "img", None, None),
            P("scene", "img", None, None),
            P("scene", "img"),
            P("scene", None, None),
            P(),
            P(),
            P("scene", None),
            P("scene", None),
            P("scene", None),
            P("scene", None),
        ),
        out_specs=(P("scene", "img", None, None), P("scene", "img", None)),
        check_vma=False,
    )
```

```python
import jax
import jax.numpy as jnp
from jax import lax
from jax.experimental import pallas as pl
from jax.experimental.pallas import tpu as pltpu
from jax.sharding import PartitionSpec as P

D = 768
HALF = D // 2
HEADS = 6
HEAD_DIM = 64
WIDTH = HEADS * HEAD_DIM
PIX = 256
TOK = 8
SLOTS = 16
SIDE = 8
IMAGES = SIDE * SIDE
RING = 4
GROUP = 16
ROWS = GROUP * TOK
WIDE = 32
MANY = WIDE * TOK
BF16 = jnp.bfloat16
F32 = jnp.float32

SHARD = 96
MID = SHARD // 2
OUT = 4 * PIX
RING_ORDER = (0, 1, 7, 2, 6, 3, 5, 4)
NEAR_FIRST = RING_ORDER[1:]
EARLY = 3


def dot(a, b):
    return jnp.dot(a, b, preferred_element_type=F32)


def dot_nt(a, b):
    return lax.dot_general(a, b, (((1,), (1,)), ((), ())), preferred_element_type=F32)


def iota(shape, dim):
    return lax.broadcasted_iota(jnp.int32, shape, dim)


def kernel(
    tok_in, pair_in, count_in, pose_in, gq_in, gk_in, wkv_in, wq_in, wo_in, wh_in,
    joined_ref, grad_ref,
    tok_s, pair_s, count_s, pose_s, gq_s, gk_s, wa, wb, wo, nkg, info_in, info, o_s, c_s, z_s, coef_s, hg, hin,
    w_send, w_recv, n_send, n_recv, i_send, i_recv, g_send, g_recv, in_sem,
):
    scene, img = lax.axis_index("scene"), lax.axis_index("img")
    x, core = scene // 2, scene % 2
    yy, zz = img // SIDE, img % SIDE
    outer = (1 - core) * yy + core * zz
    inner = (1 - core) * zz + core * yy
    myname = outer * SIDE + inner

    def img_of(o, n):
        return (1 - core) * (o * SIDE + n) + core * (n * SIDE + o)

    def turn(v, by):
        return lax.rem(v + by, SIDE)

    way = 1 - 2 * core
    right = (lax.rem(x + way + RING, RING) * 2 + core, img)
    left = (lax.rem(x - way + RING, RING) * 2 + core, img)
    twin = (x * 2 + 1 - core, img)
    in_peer = [None] + [(scene, img_of(outer, turn(inner, k))) for k in range(1, SIDE)]
    out_peer = [None] + [(scene, img_of(turn(outer, k), inner)) for k in range(1, SIDE)]

    barrier = pltpu.get_barrier_semaphore()
    peers = [peer for k in reversed(NEAR_FIRST) for peer in (in_peer[k], out_peer[k])] + [right, left, twin]

    loads = []
    row0 = pl.ds(pl.multiple_of(scene * SHARD, SHARD), SHARD)
    top = pl.ds(pl.multiple_of(scene * SHARD, 16), MID)
    bottom = pl.ds(pl.multiple_of(scene * SHARD + MID, 16), MID)
    copies = (
        (tok_in, tok_s), (gq_in, gq_s), (gk_in, gk_s), (pair_in, pair_s), (count_in, count_s),
        (pose_in, pose_s),
        (wq_in, wa.at[row0, pl.ds(0, WIDTH)]), (wkv_in, wa.at[row0, pl.ds(WIDTH, D)]),
        (wh_in, wb.at[row0, pl.ds(0, OUT)]),
        (wo_in.at[:, pl.ds(0, HALF)], wb.at[top, pl.ds(OUT, HALF)]),
        (wo_in.at[:, pl.ds(HALF, HALF)], wb.at[bottom, pl.ds(OUT, HALF)]),
    )
    for n, (src, dst) in enumerate(copies):
        copy = pltpu.make_async_copy(src, dst, in_sem.at[n])
        copy.start()
        loads.append(copy)
    for peer in peers:
        pl.semaphore_signal(barrier, inc=1, device_id=peer, device_id_type=pl.DeviceIdType.MESH)

    def remote(src, dst, send, recv, peer):
        return pltpu.make_async_remote_copy(
            src_ref=src, dst_ref=dst, send_sem=send, recv_sem=recv,
            device_id=peer, device_id_type=pl.DeviceIdType.MESH,
        )

    for copy in loads[:6]:
        copy.wait()
    xt = tok_s[0, 0].astype(F32)
    centered = xt - jnp.mean(xt, axis=-1, keepdims=True)
    normed = centered * lax.rsqrt(jnp.mean(centered * centered, axis=-1, keepdims=True) + 1e-05)
    nq = (normed * gq_s[...].reshape(1, D)).astype(BF16)
    nk = normed * gk_s[...].reshape(1, D)
    nkg[0] = jnp.concatenate([nk[:, :HALF], nk[:, HALF:]], axis=0).astype(BF16)

    lane = iota((1, 128), 1)
    first, second = pair_s[0, 0, 0:1].astype(F32), pair_s[0, 0, 1:2].astype(F32)
    live = iota((1, SLOTS), 1) < count_s[...]
    gap = jnp.full((1, 32), -1.0, F32)
    row = jnp.concatenate(
        [jnp.where(live, first, -1.0), jnp.where(live, second, -1.0), gap, second, first, gap], axis=1
    )
    tile = jnp.where(iota((SIDE, 128), 0) == inner, jnp.broadcast_to(row, (SIDE, 128)), 0.0)
    info_in[inner] = tile

    for copy in loads[6:]:
        copy.wait()
    pl.semaphore_wait(barrier, len(peers))

    gathered = (wa, wb)

    def part(p, s, lo=0, size=SHARD):
        return gathered[p].at[pl.ds(pl.multiple_of(s * SHARD + lo, 16), size)]

    def shard_of(dx, dc):
        off = -dx * way if dc else dx * way
        return lax.rem(x + off + RING, RING) * 2 + (1 - core if dc else core)

    started = []

    def send(p, n, ref, peer):
        copy = remote(ref, ref, w_send.at[p, n], w_recv.at[p, n], peer)
        copy.start()
        started.append(copy)

    def got(p, n, ref):
        remote(ref, ref, w_send.at[p, n], w_recv.at[p, n], twin).wait_recv()

    def own(p):
        for n, peer in enumerate((right, left, twin)):
            send(p, n, part(p, scene), peer)

    def near(p):
        got(p, 0, part(p, shard_of(-1, 0)))
        send(p, 3, part(p, shard_of(-1, 0), 0, MID), right)
        send(p, 5, part(p, shard_of(-1, 0)), twin)
        got(p, 1, part(p, shard_of(1, 0)))
        send(p, 4, part(p, shard_of(1, 0), MID, MID), left)
        send(p, 6, part(p, shard_of(1, 0)), twin)

    def far(p):
        got(p, 3, part(p, shard_of(2, 0), 0, MID))
        send(p, 7, part(p, shard_of(2, 0), 0, MID), twin)
        got(p, 4, part(p, shard_of(2, 0), MID, MID))
        send(p, 8, part(p, shard_of(2, 0), MID, MID), twin)

    def finish(p):
        got(p, 2, part(p, shard_of(0, 1)))
        got(p, 5, part(p, shard_of(-1, 1)))
        got(p, 6, part(p, shard_of(1, 1)))
        got(p, 7, part(p, shard_of(2, 1), 0, MID))
        got(p, 8, part(p, shard_of(2, 1), MID, MID))

    low = inner % 2 * MID
    twin_low = outer % 2 * MID
    partner = (scene, img_of(outer, inner + 1 - 2 * (inner % 2)))

    def some(s, base, off, size):
        return wa.at[pl.ds(pl.multiple_of(s * SHARD + base + off, 16), size)]

    def fetched(dc, base):
        return (
            some(shard_of(-1, dc), base, 0, MID), some(shard_of(1, dc), base, 0, MID),
            some(shard_of(2, dc), base, 0, 32), some(shard_of(2, dc), base, 32, 16),
        )

    ours, swapped = fetched(0, low), fetched(0, MID - low)
    theirs = fetched(1, twin_low) + fetched(1, MID - twin_low)

    def own_half():
        half = some(scene, low, 0, MID)
        send(0, 0, half, right)
        send(0, 1, half, left)
        send(0, 2, part(0, scene), twin)

    def near_half():
        got(0, 0, ours[0])
        send(0, 3, some(shard_of(-1, 0), low, 0, 32), right)
        send(0, 9, ours[0], partner)
        send(0, 5, ours[0], twin)
        got(0, 1, ours[1])
        send(0, 4, some(shard_of(1, 0), low, 32, 16), left)
        send(0, 10, ours[1], partner)
        send(0, 6, ours[1], twin)

    def far_half():
        for n in (2, 3):
            got(0, 1 + n, ours[n])
            send(0, 9 + n, ours[n], partner)
            send(0, 5 + n, ours[n], twin)

    def swap_half():
        for n in range(4):
            got(0, 9 + n, swapped[n])
            send(0, 13 + n, swapped[n], twin)

    def finish_half():
        got(0, 2, part(0, shard_of(0, 1)))
        for n in range(4):
            got(0, 5 + n, theirs[n])
            got(0, 13 + n, theirs[4 + n])

    own_half()
    for k in reversed(NEAR_FIRST):
        slot = nkg.at[RING_ORDER.index(k)]
        copy = remote(nkg.at[0], slot, n_send.at[0, k], n_recv.at[0, k], in_peer[k])
        copy.start()
        started.append(copy)
    own(1)
    for k in reversed(NEAR_FIRST):
        slot = info_in.at[inner]
        copy = remote(slot, slot, i_send.at[0, k], i_recv.at[0, k], in_peer[k])
        copy.start()
        started.append(copy)

    def arrive(k):
        slot = nkg.at[RING_ORDER.index(k)]
        remote(slot, slot, n_send.at[0, k], n_recv.at[0, k], in_peer[k]).wait_recv()

    def pass_on(lo, size):
        group = nkg.at[pl.ds(lo, size)]
        for k in reversed(NEAR_FIRST):
            there = nkg.at[pl.ds(RING_ORDER.index(k) * SIDE + lo, size)]
            remote(group, there, n_send.at[1, k], n_recv.at[1, k], out_peer[k]).start()

    for k in RING_ORDER[1:EARLY]:
        arrive(k)
    pass_on(0, EARLY)
    for k in RING_ORDER[EARLY:]:
        arrive(k)
    for k in NEAR_FIRST:
        slot = info_in.at[turn(inner, SIDE - k)]
        remote(slot, slot, i_send.at[0, k], i_recv.at[0, k], in_peer[k]).wait_recv()
    total = info_in[0]
    for k in range(1, SIDE):
        total = total + info_in[k]
    info[outer] = total
    for k in reversed(NEAR_FIRST):
        copy = remote(info.at[outer], info.at[outer], i_send.at[1, k], i_recv.at[1, k], out_peer[k])
        copy.start()
        started.append(copy)
    pass_on(EARLY, SIDE - EARLY)
    near_half()
    near(1)
    far_half()

    for k in range(1, SIDE):
        slot = turn(outer, SIDE - k)
        remote(info.at[slot], info.at[slot], i_send.at[1, k], i_recv.at[1, k], out_peer[k]).wait_recv()
    table = info[...].reshape(IMAGES, 128)
    partner = pltpu.roll(table, 64, 1) + 1.0
    lanes = iota((IMAGES, 128), 1)
    match = table == img.astype(F32)
    ones = jnp.ones((SIDE, 128), F32)
    as_first = dot_nt(ones, jnp.where(match & (lanes < 16), partner, 0.0))
    as_second = dot_nt(ones, jnp.where(match & (lanes >= 16) & (lanes < 32), partner, 0.0))
    pos_row = iota((IMAGES, IMAGES), 0)
    pos_col = iota((IMAGES, IMAGES), 1)
    def back(slot):
        return (slot % 2) * ((slot + 1) // 2) + (1 - slot % 2) * (SIDE - slot // 2)

    at_outer = (outer - back(pos_row // SIDE) + 2 * SIDE) % SIDE
    at_inner = (inner - back(pos_row % SIDE) + 2 * SIDE) % SIDE
    image_at = (1 - core) * (at_outer * SIDE + at_inner) + core * (at_inner * SIDE + at_outer)
    name = (image_at + 1).astype(F32)
    m1 = jnp.sum(jnp.where(as_first[0:1] == name, 1.0, 0.0), axis=1, keepdims=True)
    m2 = jnp.sum(jnp.where(as_second[0:1] == name, 1.0, 0.0), axis=1, keepdims=True)
    pose = jnp.concatenate(
        [pose_s[:, 0], jnp.ones((1, IMAGES), F32), jnp.zeros((115, IMAGES), F32)], axis=0
    )
    number = iota((128, IMAGES), 0)
    pose = pose + jnp.where((number == 0) | (number == 4) | (number == 8), 1.0, 0.0)
    pose = lax.dot_general(
        jnp.where(image_at == pos_col, 1.0, 0.0), pose, (((1,), (1,)), ((), ())),
        precision=lax.Precision.HIGHEST, preferred_element_type=F32,
    )
    mine = pose[0:1]
    coef = m1 * mine + m2 * pose
    coef_s[...] = jnp.broadcast_to(coef[:, None, :], (IMAGES, TOK, 128)).reshape(IMAGES * TOK, 128)

    swap_half()

    def tokens_in(k, slot):
        group = nkg.at[pl.ds(slot * SIDE, SIDE)]
        remote(group, group, n_send.at[1, k], n_recv.at[1, k], out_peer[1]).wait_recv()

    finish_half()
    q = dot(nq, wa[:, :WIDTH]).astype(BF16).astype(F32) * HEAD_DIM ** (-0.5)
    qbig = jnp.concatenate([q] * HEADS, axis=0)
    own_head = iota((HEADS * TOK, WIDTH), 0) // TOK == iota((HEADS * TOK, WIDTH), 1) // HEAD_DIM
    qbig = jnp.where(own_head, qbig, 0.0).astype(BF16)
    same = iota((ROWS, ROWS), 0) // TOK == iota((ROWS, ROWS), 1) // TOK
    head_of = iota((ROWS, WIDTH), 1) // HEAD_DIM
    x_tile = jnp.concatenate([xt] * WIDE, axis=0)

    tokens_in(1, 1)

    def attend(g, carry):
        rows = pl.ds(pl.multiple_of(g * ROWS, ROWS), ROWS)
        block = nkg[pl.ds(g * GROUP, GROUP)].astype(F32)
        low = block[:, :TOK].reshape(ROWS, HALF).astype(BF16)
        high = block[:, TOK:].reshape(ROWS, HALF).astype(BF16)
        kv = dot(low, wa[:HALF, WIDTH:]) + dot(high, wa[HALF:, WIDTH:])
        keys = kv[:, :WIDTH].astype(BF16)
        values = kv[:, WIDTH:].astype(BF16).astype(F32)
        scores = dot_nt(keys, qbig).reshape(GROUP, TOK, HEADS * TOK)
        e = jnp.exp(scores - jnp.max(scores, axis=1, keepdims=True))
        attn = (e / jnp.sum(e, axis=1, keepdims=True)).reshape(ROWS, HEADS * TOK)
        turned = attn.T
        spread = []
        for h in range(HEADS):
            piece = jnp.concatenate([turned[h * TOK:(h + 1) * TOK]] * GROUP, axis=0)
            spread.append(jnp.where(same, piece, 0.0).astype(BF16))
        split = [jnp.where(head_of == h, values, 0.0).astype(BF16) for h in range(HEADS)]
        o = dot(jnp.concatenate(spread, axis=1), jnp.concatenate(split, axis=0))
        o_s[rows] = o.astype(BF16)

        @pl.when(g < IMAGES // GROUP - 1)
        def _():
            tokens_in(SIDE - 1 - g, 2 * g + 2)
            tokens_in(g + 2, 2 * g + 3)

        return carry

    lax.fori_loop(0, 1, attend, 0)
    far(1)
    lax.fori_loop(1, IMAGES // GROUP, attend, 0)
    finish(1)
    for s in range(D // SHARD):
        wo[s * MID:(s + 1) * MID, :HALF] = wb[s * SHARD:s * SHARD + MID, OUT:]
        wo[s * MID:(s + 1) * MID, HALF:] = wb[s * SHARD + MID:(s + 1) * SHARD, OUT:]

    def points(g, carry):
        rows = pl.ds(pl.multiple_of(g * MANY, MANY), MANY)
        y = (x_tile + dot(o_s[rows], wo[...])).astype(BF16)
        r = dot(y, wb[:, :OUT])
        cf = coef_s[rows]
        conf = 1.0 + jnp.exp(jnp.where(cf[:, 12:13] > 0.0, r[:, 3 * PIX:], 0.0))
        pts = [conf * r[:, k * PIX:(k + 1) * PIX] for k in range(3)]
        c_s[rows] = conf
        for n, value in enumerate(pts + [conf]):
            z_s[n, rows] = value[:, :128] + value[:, 128:]
        new = []
        for k in range(3):
            w = cf[:, 9 + k:10 + k] * conf
            for m in range(3):
                w = w + cf[:, 3 * k + m:3 * k + m + 1] * pts[m]
            new.append(carry[k] + jnp.sum(w.reshape(WIDE, TOK, PIX), axis=0))
        w = cf[:, 12:13] * conf
        new.append(carry[3] + jnp.sum(w.reshape(WIDE, TOK, PIX), axis=0))
        return tuple(new)

    zero = jnp.zeros((TOK, PIX), F32)
    sums = lax.fori_loop(0, IMAGES // WIDE, points, (zero,) * 4)
    joined = [(sums[k] / sums[3]).astype(BF16).astype(F32) for k in range(3)]
    joined_rows = [jnp.concatenate([j[t:t + 1] for t in range(TOK)], axis=1) for j in joined]
    joined_ref[0, 0] = jnp.concatenate(joined_rows, axis=0).astype(BF16)

    conf = c_s[...]
    coarse = conf.astype(BF16)
    fine = (conf - coarse.astype(F32)).astype(BF16)
    target = jnp.concatenate(joined, axis=0).astype(BF16)
    cross = dot_nt(coarse, target) + dot_nt(fine, target)
    agree = iota((IMAGES * TOK, 3 * TOK), 0) % TOK == iota((IMAGES * TOK, 3 * TOK), 1) % TOK
    cross = jnp.sum(jnp.where(agree, cross, 0.0).reshape(IMAGES, TOK, 3 * TOK), axis=1)
    channel = iota((IMAGES, 3 * TOK), 1) // TOK
    met = [jnp.sum(jnp.where(channel == k, cross, 0.0), axis=1, keepdims=True) for k in range(3)]
    total = [
        jnp.sum(jnp.sum(z_s[n].reshape(IMAGES, TOK, 128), axis=1), axis=1, keepdims=True)
        for n in range(4)
    ]
    sent = jnp.zeros((IMAGES, 128), F32)
    kept = jnp.zeros((1, 128), F32)
    for k in range(3):
        theirs = pose[:, 9 + k:10 + k] * total[3] - met[k]
        ours = mine[:, 9 + k:10 + k] * total[3] - met[k]
        for m in range(3):
            theirs = theirs + pose[:, 3 * k + m:3 * k + m + 1] * total[m]
            ours = ours + mine[:, 3 * k + m:3 * k + m + 1] * total[m]
        sent = jnp.where(lanes == k, m2 * theirs, sent)
        kept = jnp.where(lane == k, jnp.sum(m1 * ours, axis=0, keepdims=True), kept)
    by_inner = [(1 - core) * turn(inner, k) + core * SIDE * turn(inner, k) for k in range(SIDE)]
    hg[...] = sent.reshape(IMAGES, 1, 128)

    for far_out in reversed(RING_ORDER):
        to = turn(outer, far_out)
        by_outer = (1 - core) * to * SIDE + core * to
        row_of = RING_ORDER.index((SIDE - far_out) % SIDE) * SIDE
        for k in reversed(RING_ORDER):
            if far_out == 0 and k == 0:
                continue
            src = hg.at[row_of + RING_ORDER.index((SIDE - k) % SIDE)]
            remote(src, hin.at[myname], g_send.at[0], g_recv.at[0], (scene, by_outer + by_inner[k])).start()
    hin[myname] = jnp.zeros((1, 128), F32)
    for copy in started:
        copy.wait_send()
    all_tokens = nkg.at[pl.ds(0, SIDE)]
    for k in range(1, SIDE):
        remote(all_tokens, all_tokens, n_send.at[1, k], n_recv.at[1, k], out_peer[k]).wait_send()
    most = hin.at[pl.ds(0, IMAGES - 1)]
    exchange = remote(most, most, g_send.at[0], g_recv.at[0], twin)
    exchange.wait_send()
    exchange.wait_recv()
    row = jnp.sum(hin[...], axis=0)
    grad_ref[0] = ((row + kept) * (2.0 / (TOK * PIX)))[:, :3]


def on_device(
    tokens, pair_list, pair_count, poses, gain_query, gain_kv, w_query, w_kv, w_out, w_head
):
    vmem = pl.BlockSpec(memory_space=pltpu.VMEM)
    hbm = pl.BlockSpec(memory_space=pltpu.HBM)
    dma = pltpu.SemaphoreType.DMA
    return pl.pallas_call(
        kernel,
        out_shape=(
            jax.ShapeDtypeStruct((1, 1, 3, TOK * PIX), BF16),
            jax.ShapeDtypeStruct((1, 1, 3), F32),
        ),
        in_specs=[hbm] * 10,
        out_specs=(vmem, vmem),
        scratch_shapes=[
            pltpu.VMEM((1, 1, TOK, D), BF16),
            pltpu.VMEM((1, 1, 2, SLOTS), jnp.int32),
            pltpu.VMEM((1, 1), jnp.int32),
            pltpu.VMEM((12, 1, IMAGES), F32),
            pltpu.VMEM((D,), F32),
            pltpu.VMEM((D,), F32),
            pltpu.VMEM((D, WIDTH + D), BF16),
            pltpu.VMEM((D, OUT + HALF), BF16),
            pltpu.VMEM((WIDTH, D), BF16),
            pltpu.VMEM((IMAGES, 2 * TOK, HALF), BF16),
            pltpu.VMEM((SIDE, SIDE, 128), F32),
            pltpu.VMEM((SIDE, SIDE, 128), F32),
            pltpu.VMEM((IMAGES * TOK, WIDTH), BF16),
            pltpu.VMEM((IMAGES * TOK, PIX), F32),
            pltpu.VMEM((4, IMAGES * TOK, 128), F32),
            pltpu.VMEM((IMAGES * TOK, 128), F32),
            pltpu.VMEM((IMAGES, 1, 128), F32),
            pltpu.VMEM((IMAGES, 1, 128), F32),
            dma((2, 17)),
            dma((2, 17)),
            dma((2, SIDE)),
            dma((2, SIDE)),
            dma((2, SIDE)),
            dma((2, SIDE)),
            dma((1,)),
            dma((1,)),
            dma((11,)),
        ],
        compiler_params=pltpu.CompilerParams(
            collective_id=0, has_side_effects=True, vmem_limit_bytes=64 * 1024 * 1024
        ),
    )(
        tokens, jnp.swapaxes(pair_list, 2, 3), pair_count, jnp.transpose(poses, (2, 0, 1)),
        gain_query, gain_kv, w_kv, w_query, w_out, w_head,
    )


def solution(mesh):
    return jax.shard_map(
        on_device,
        mesh=mesh,
        in_specs=(
            P("scene", "img", None, None),
            P("scene", "img", None, None),
            P("scene", "img"),
            P("scene", None, None),
            P(),
            P(),
            P("scene", None),
            P("scene", None),
            P("scene", None),
            P("scene", None),
        ),
        out_specs=(P("scene", "img", None, None), P("scene", "img", None)),
        check_vma=False,
    )
```

```python
import jax
import jax.numpy as jnp
from jax import lax
from jax.experimental import pallas as pl
from jax.experimental.pallas import tpu as pltpu
from jax.sharding import PartitionSpec as P

D = 768
HALF = D // 2
HEADS = 6
HEAD_DIM = 64
WIDTH = HEADS * HEAD_DIM
PIX = 256
TOK = 8
SLOTS = 16
SIDE = 8
IMAGES = SIDE * SIDE
RING = 4
GROUP = 16
ROWS = GROUP * TOK
WIDE = 32
MANY = WIDE * TOK
BF16 = jnp.bfloat16
F32 = jnp.float32

SHARD = 96
MID = SHARD // 2
OUT = 4 * PIX
RING_ORDER = (0, 1, 7, 2, 6, 3, 5, 4)
NEAR_FIRST = RING_ORDER[1:]
EARLY = 3


def dot(a, b):
    return jnp.dot(a, b, preferred_element_type=F32)


def dot_nt(a, b):
    return lax.dot_general(a, b, (((1,), (1,)), ((), ())), preferred_element_type=F32)


def iota(shape, dim):
    return lax.broadcasted_iota(jnp.int32, shape, dim)


def kernel(
    tok_in, pair_in, count_in, pose_in, gq_in, gk_in, wkv_in, wq_in, wo_in, wh_in,
    joined_ref, grad_ref,
    tok_s, pair_s, count_s, pose_s, gq_s, gk_s, wa, wb, wo, nkg, info_in, info, o_s, c_s, z_s, coef_s, hg, hin,
    w_send, w_recv, n_send, n_recv, i_send, i_recv, g_send, g_recv, in_sem,
):
    scene, img = lax.axis_index("scene"), lax.axis_index("img")
    x, core = scene // 2, scene % 2
    yy, zz = img // SIDE, img % SIDE
    outer = (1 - core) * yy + core * zz
    inner = (1 - core) * zz + core * yy
    myname = outer * SIDE + inner

    def img_of(o, n):
        return (1 - core) * (o * SIDE + n) + core * (n * SIDE + o)

    def turn(v, by):
        return lax.rem(v + by, SIDE)

    way = 1 - 2 * core
    right = (lax.rem(x + way + RING, RING) * 2 + core, img)
    left = (lax.rem(x - way + RING, RING) * 2 + core, img)
    twin = (x * 2 + 1 - core, img)
    in_peer = [None] + [(scene, img_of(outer, turn(inner, k))) for k in range(1, SIDE)]
    out_peer = [None] + [(scene, img_of(turn(outer, k), inner)) for k in range(1, SIDE)]

    barrier = pltpu.get_barrier_semaphore()
    peers = [peer for k in reversed(NEAR_FIRST) for peer in (in_peer[k], out_peer[k])] + [right, left, twin]

    loads = []
    row0 = pl.ds(pl.multiple_of(scene * SHARD, SHARD), SHARD)
    top = pl.ds(pl.multiple_of(scene * SHARD, 16), MID)
    bottom = pl.ds(pl.multiple_of(scene * SHARD + MID, 16), MID)
    copies = (
        (tok_in, tok_s), (gq_in, gq_s), (gk_in, gk_s), (pair_in, pair_s), (count_in, count_s),
        (pose_in, pose_s),
        (wq_in, wa.at[row0, pl.ds(0, WIDTH)]), (wkv_in, wa.at[row0, pl.ds(WIDTH, D)]),
        (wh_in, wb.at[row0, pl.ds(0, OUT)]),
        (wo_in.at[:, pl.ds(0, HALF)], wb.at[top, pl.ds(OUT, HALF)]),
        (wo_in.at[:, pl.ds(HALF, HALF)], wb.at[bottom, pl.ds(OUT, HALF)]),
    )
    for n, (src, dst) in enumerate(copies):
        copy = pltpu.make_async_copy(src, dst, in_sem.at[n])
        copy.start()
        loads.append(copy)
    for peer in peers:
        pl.semaphore_signal(barrier, inc=1, device_id=peer, device_id_type=pl.DeviceIdType.MESH)

    def remote(src, dst, send, recv, peer):
        return pltpu.make_async_remote_copy(
            src_ref=src, dst_ref=dst, send_sem=send, recv_sem=recv,
            device_id=peer, device_id_type=pl.DeviceIdType.MESH,
        )

    for copy in loads[:6]:
        copy.wait()
    xt = tok_s[0, 0].astype(F32)
    centered = xt - jnp.mean(xt, axis=-1, keepdims=True)
    normed = centered * lax.rsqrt(jnp.mean(centered * centered, axis=-1, keepdims=True) + 1e-05)
    nq = (normed * gq_s[...].reshape(1, D)).astype(BF16)
    nk = normed * gk_s[...].reshape(1, D)
    nkg[0] = jnp.concatenate([nk[:, :HALF], nk[:, HALF:]], axis=0).astype(BF16)

    lane = iota((1, 128), 1)
    first, second = pair_s[0, 0, 0:1].astype(F32), pair_s[0, 0, 1:2].astype(F32)
    live = iota((1, SLOTS), 1) < count_s[...]
    gap = jnp.full((1, 32), -1.0, F32)
    row = jnp.concatenate(
        [jnp.where(live, first, -1.0), jnp.where(live, second, -1.0), gap, second, first, gap], axis=1
    )
    tile = jnp.where(iota((SIDE, 128), 0) == inner, jnp.broadcast_to(row, (SIDE, 128)), 0.0)
    info_in[inner] = tile

    for copy in loads[6:]:
        copy.wait()
    pl.semaphore_wait(barrier, len(peers))

    gathered = (wa, wb)

    def part(p, s, lo=0, size=SHARD):
        return gathered[p].at[pl.ds(pl.multiple_of(s * SHARD + lo, 16), size)]

    def shard_of(dx, dc):
        off = -dx * way if dc else dx * way
        return lax.rem(x + off + RING, RING) * 2 + (1 - core if dc else core)

    started = []

    def send(p, n, ref, peer):
        copy = remote(ref, ref, w_send.at[p, n], w_recv.at[p, n], peer)
        copy.start()
        started.append(copy)

    def got(p, n, ref):
        remote(ref, ref, w_send.at[p, n], w_recv.at[p, n], twin).wait_recv()

    def own(p):
        for n, peer in enumerate((right, left, twin)):
            send(p, n, part(p, scene), peer)

    def near(p):
        got(p, 0, part(p, shard_of(-1, 0)))
        send(p, 3, part(p, shard_of(-1, 0), 0, MID), right)
        send(p, 5, part(p, shard_of(-1, 0)), twin)
        got(p, 1, part(p, shard_of(1, 0)))
        send(p, 4, part(p, shard_of(1, 0), MID, MID), left)
        send(p, 6, part(p, shard_of(1, 0)), twin)

    def far(p):
        got(p, 3, part(p, shard_of(2, 0), 0, MID))
        send(p, 7, part(p, shard_of(2, 0), 0, MID), twin)
        got(p, 4, part(p, shard_of(2, 0), MID, MID))
        send(p, 8, part(p, shard_of(2, 0), MID, MID), twin)

    def finish(p):
        got(p, 2, part(p, shard_of(0, 1)))
        got(p, 5, part(p, shard_of(-1, 1)))
        got(p, 6, part(p, shard_of(1, 1)))
        got(p, 7, part(p, shard_of(2, 1), 0, MID))
        got(p, 8, part(p, shard_of(2, 1), MID, MID))

    low = inner % 2 * MID
    twin_low = outer % 2 * MID
    partner = (scene, img_of(outer, inner + 1 - 2 * (inner % 2)))

    def some(s, base, off, size):
        return wa.at[pl.ds(pl.multiple_of(s * SHARD + base + off, 16), size)]

    def fetched(dc, base):
        return (
            some(shard_of(-1, dc), base, 0, MID), some(shard_of(1, dc), base, 0, MID),
            some(shard_of(2, dc), base, 0, 32), some(shard_of(2, dc), base, 32, 16),
        )

    ours, swapped = fetched(0, low), fetched(0, MID - low)
    theirs = fetched(1, twin_low) + fetched(1, MID - twin_low)

    def own_half():
        half = some(scene, low, 0, MID)
        send(0, 0, half, right)
        send(0, 1, half, left)
        send(0, 2, part(0, scene), twin)

    def near_half():
        got(0, 0, ours[0])
        send(0, 3, some(shard_of(-1, 0), low, 0, 32), right)
        send(0, 9, ours[0], partner)
        send(0, 5, ours[0], twin)
        got(0, 1, ours[1])
        send(0, 4, some(shard_of(1, 0), low, 32, 16), left)
        send(0, 10, ours[1], partner)
        send(0, 6, ours[1], twin)

    def far_half():
        for n in (2, 3):
            got(0, 1 + n, ours[n])
            send(0, 9 + n, ours[n], partner)
            send(0, 5 + n, ours[n], twin)

    def swap_half():
        for n in range(4):
            got(0, 9 + n, swapped[n])
            send(0, 13 + n, swapped[n], twin)

    def finish_half():
        got(0, 2, part(0, shard_of(0, 1)))
        for n in range(4):
            got(0, 5 + n, theirs[n])
            got(0, 13 + n, theirs[4 + n])

    for k in reversed(NEAR_FIRST):
        slot = nkg.at[RING_ORDER.index(k)]
        copy = remote(nkg.at[0], slot, n_send.at[0, k], n_recv.at[0, k], in_peer[k])
        copy.start()
        started.append(copy)
    own_half()
    own(1)
    for k in reversed(NEAR_FIRST):
        slot = info_in.at[inner]
        copy = remote(slot, slot, i_send.at[0, k], i_recv.at[0, k], in_peer[k])
        copy.start()
        started.append(copy)

    def arrive(k):
        slot = nkg.at[RING_ORDER.index(k)]
        remote(slot, slot, n_send.at[0, k], n_recv.at[0, k], in_peer[k]).wait_recv()

    def pass_on(lo, size):
        group = nkg.at[pl.ds(lo, size)]
        for k in reversed(NEAR_FIRST):
            there = nkg.at[pl.ds(RING_ORDER.index(k) * SIDE + lo, size)]
            remote(group, there, n_send.at[1, k], n_recv.at[1, k], out_peer[k]).start()

    for k in RING_ORDER[1:EARLY]:
        arrive(k)
    pass_on(0, EARLY)
    for k in RING_ORDER[EARLY:]:
        arrive(k)
    for k in NEAR_FIRST:
        slot = info_in.at[turn(inner, SIDE - k)]
        remote(slot, slot, i_send.at[0, k], i_recv.at[0, k], in_peer[k]).wait_recv()
    total = info_in[0]
    for k in range(1, SIDE):
        total = total + info_in[k]
    info[outer] = total
    for k in reversed(NEAR_FIRST):
        copy = remote(info.at[outer], info.at[outer], i_send.at[1, k], i_recv.at[1, k], out_peer[k])
        copy.start()
        started.append(copy)
    pass_on(EARLY, SIDE - EARLY)
    near_half()
    near(1)
    far_half()

    for k in range(1, SIDE):
        slot = turn(outer, SIDE - k)
        remote(info.at[slot], info.at[slot], i_send.at[1, k], i_recv.at[1, k], out_peer[k]).wait_recv()
    table = info[...].reshape(IMAGES, 128)
    partner = pltpu.roll(table, 64, 1) + 1.0
    lanes = iota((IMAGES, 128), 1)
    match = table == img.astype(F32)
    ones = jnp.ones((SIDE, 128), F32)
    as_first = dot_nt(ones, jnp.where(match & (lanes < 16), partner, 0.0))
    as_second = dot_nt(ones, jnp.where(match & (lanes >= 16) & (lanes < 32), partner, 0.0))
    pos_row = iota((IMAGES, IMAGES), 0)
    pos_col = iota((IMAGES, IMAGES), 1)
    def back(slot):
        return (slot % 2) * ((slot + 1) // 2) + (1 - slot % 2) * (SIDE - slot // 2)

    at_outer = (outer - back(pos_row // SIDE) + 2 * SIDE) % SIDE
    at_inner = (inner - back(pos_row % SIDE) + 2 * SIDE) % SIDE
    image_at = (1 - core) * (at_outer * SIDE + at_inner) + core * (at_inner * SIDE + at_outer)
    name = (image_at + 1).astype(F32)
    m1 = jnp.sum(jnp.where(as_first[0:1] == name, 1.0, 0.0), axis=1, keepdims=True)
    m2 = jnp.sum(jnp.where(as_second[0:1] == name, 1.0, 0.0), axis=1, keepdims=True)
    pose = jnp.concatenate(
        [pose_s[:, 0], jnp.ones((1, IMAGES), F32), jnp.zeros((115, IMAGES), F32)], axis=0
    )
    number = iota((128, IMAGES), 0)
    pose = pose + jnp.where((number == 0) | (number == 4) | (number == 8), 1.0, 0.0)
    pose = lax.dot_general(
        jnp.where(image_at == pos_col, 1.0, 0.0), pose, (((1,), (1,)), ((), ())),
        precision=lax.Precision.HIGHEST, preferred_element_type=F32,
    )
    mine = pose[0:1]
    coef = m1 * mine + m2 * pose
    coef_s[...] = jnp.broadcast_to(coef[:, None, :], (IMAGES, TOK, 128)).reshape(IMAGES * TOK, 128)

    swap_half()

    def tokens_in(k, slot):
        group = nkg.at[pl.ds(slot * SIDE, SIDE)]
        remote(group, group, n_send.at[1, k], n_recv.at[1, k], out_peer[1]).wait_recv()

    finish_half()
    q = dot(nq, wa[:, :WIDTH]).astype(BF16).astype(F32) * HEAD_DIM ** (-0.5)
    qbig = jnp.concatenate([q] * HEADS, axis=0)
    own_head = iota((HEADS * TOK, WIDTH), 0) // TOK == iota((HEADS * TOK, WIDTH), 1) // HEAD_DIM
    qbig = jnp.where(own_head, qbig, 0.0).astype(BF16)
    same = iota((ROWS, ROWS), 0) // TOK == iota((ROWS, ROWS), 1) // TOK
    head_of = iota((ROWS, WIDTH), 1) // HEAD_DIM
    x_tile = jnp.concatenate([xt] * WIDE, axis=0)

    tokens_in(1, 1)

    def attend(g, carry):
        rows = pl.ds(pl.multiple_of(g * ROWS, ROWS), ROWS)
        block = nkg[pl.ds(g * GROUP, GROUP)].astype(F32)
        low = block[:, :TOK].reshape(ROWS, HALF).astype(BF16)
        high = block[:, TOK:].reshape(ROWS, HALF).astype(BF16)
        kv = dot(low, wa[:HALF, WIDTH:]) + dot(high, wa[HALF:, WIDTH:])
        keys = kv[:, :WIDTH].astype(BF16)
        values = kv[:, WIDTH:].astype(BF16).astype(F32)
        scores = dot_nt(keys, qbig).reshape(GROUP, TOK, HEADS * TOK)
        e = jnp.exp(scores - jnp.max(scores, axis=1, keepdims=True))
        attn = (e / jnp.sum(e, axis=1, keepdims=True)).reshape(ROWS, HEADS * TOK)
        turned = attn.T
        spread = []
        for h in range(HEADS):
            piece = jnp.concatenate([turned[h * TOK:(h + 1) * TOK]] * GROUP, axis=0)
            spread.append(jnp.where(same, piece, 0.0).astype(BF16))
        split = [jnp.where(head_of == h, values, 0.0).astype(BF16) for h in range(HEADS)]
        o = dot(jnp.concatenate(spread, axis=1), jnp.concatenate(split, axis=0))
        o_s[rows] = o.astype(BF16)

        @pl.when(g < IMAGES // GROUP - 1)
        def _():
            tokens_in(SIDE - 1 - g, 2 * g + 2)
            tokens_in(g + 2, 2 * g + 3)

        return carry

    far(1)
    lax.fori_loop(0, IMAGES // GROUP, attend, 0)
    finish(1)
    for s in range(D // SHARD):
        wo[s * MID:(s + 1) * MID, :HALF] = wb[s * SHARD:s * SHARD + MID, OUT:]
        wo[s * MID:(s + 1) * MID, HALF:] = wb[s * SHARD + MID:(s + 1) * SHARD, OUT:]

    def points(g, carry):
        rows = pl.ds(pl.multiple_of(g * MANY, MANY), MANY)
        y = (x_tile + dot(o_s[rows], wo[...])).astype(BF16)
        r = dot(y, wb[:, :OUT])
        cf = coef_s[rows]
        conf = 1.0 + jnp.exp(jnp.where(cf[:, 12:13] > 0.0, r[:, 3 * PIX:], 0.0))
        pts = [conf * r[:, k * PIX:(k + 1) * PIX] for k in range(3)]
        c_s[rows] = conf
        for n, value in enumerate(pts + [conf]):
            z_s[n, rows] = value[:, :128] + value[:, 128:]
        new = []
        for k in range(3):
            w = cf[:, 9 + k:10 + k] * conf
            for m in range(3):
                w = w + cf[:, 3 * k + m:3 * k + m + 1] * pts[m]
            new.append(carry[k] + jnp.sum(w.reshape(WIDE, TOK, PIX), axis=0))
        w = cf[:, 12:13] * conf
        new.append(carry[3] + jnp.sum(w.reshape(WIDE, TOK, PIX), axis=0))
        return tuple(new)

    zero = jnp.zeros((TOK, PIX), F32)
    sums = lax.fori_loop(0, IMAGES // WIDE, points, (zero,) * 4)
    joined = [(sums[k] / sums[3]).astype(BF16).astype(F32) for k in range(3)]
    joined_rows = [jnp.concatenate([j[t:t + 1] for t in range(TOK)], axis=1) for j in joined]
    joined_ref[0, 0] = jnp.concatenate(joined_rows, axis=0).astype(BF16)

    conf = c_s[...]
    coarse = conf.astype(BF16)
    fine = (conf - coarse.astype(F32)).astype(BF16)
    target = jnp.concatenate(joined, axis=0).astype(BF16)
    cross = dot_nt(coarse, target) + dot_nt(fine, target)
    agree = iota((IMAGES * TOK, 3 * TOK), 0) % TOK == iota((IMAGES * TOK, 3 * TOK), 1) % TOK
    cross = jnp.sum(jnp.where(agree, cross, 0.0).reshape(IMAGES, TOK, 3 * TOK), axis=1)
    channel = iota((IMAGES, 3 * TOK), 1) // TOK
    met = [jnp.sum(jnp.where(channel == k, cross, 0.0), axis=1, keepdims=True) for k in range(3)]
    total = [
        jnp.sum(jnp.sum(z_s[n].reshape(IMAGES, TOK, 128), axis=1), axis=1, keepdims=True)
        for n in range(4)
    ]
    sent = jnp.zeros((IMAGES, 128), F32)
    kept = jnp.zeros((1, 128), F32)
    for k in range(3):
        theirs = pose[:, 9 + k:10 + k] * total[3] - met[k]
        ours = mine[:, 9 + k:10 + k] * total[3] - met[k]
        for m in range(3):
            theirs = theirs + pose[:, 3 * k + m:3 * k + m + 1] * total[m]
            ours = ours + mine[:, 3 * k + m:3 * k + m + 1] * total[m]
        sent = jnp.where(lanes == k, m2 * theirs, sent)
        kept = jnp.where(lane == k, jnp.sum(m1 * ours, axis=0, keepdims=True), kept)
    by_inner = [(1 - core) * turn(inner, k) + core * SIDE * turn(inner, k) for k in range(SIDE)]
    hg[...] = sent.reshape(IMAGES, 1, 128)

    for far_out in reversed(RING_ORDER):
        to = turn(outer, far_out)
        by_outer = (1 - core) * to * SIDE + core * to
        row_of = RING_ORDER.index((SIDE - far_out) % SIDE) * SIDE
        for k in reversed(RING_ORDER):
            if far_out == 0 and k == 0:
                continue
            src = hg.at[row_of + RING_ORDER.index((SIDE - k) % SIDE)]
            remote(src, hin.at[myname], g_send.at[0], g_recv.at[0], (scene, by_outer + by_inner[k])).start()
    hin[myname] = jnp.zeros((1, 128), F32)
    for copy in started:
        copy.wait_send()
    all_tokens = nkg.at[pl.ds(0, SIDE)]
    for k in range(1, SIDE):
        remote(all_tokens, all_tokens, n_send.at[1, k], n_recv.at[1, k], out_peer[k]).wait_send()
    most = hin.at[pl.ds(0, IMAGES - 1)]
    exchange = remote(most, most, g_send.at[0], g_recv.at[0], twin)
    exchange.wait_send()
    exchange.wait_recv()
    row = jnp.sum(hin[...], axis=0)
    grad_ref[0] = ((row + kept) * (2.0 / (TOK * PIX)))[:, :3]


def on_device(
    tokens, pair_list, pair_count, poses, gain_query, gain_kv, w_query, w_kv, w_out, w_head
):
    vmem = pl.BlockSpec(memory_space=pltpu.VMEM)
    hbm = pl.BlockSpec(memory_space=pltpu.HBM)
    dma = pltpu.SemaphoreType.DMA
    return pl.pallas_call(
        kernel,
        out_shape=(
            jax.ShapeDtypeStruct((1, 1, 3, TOK * PIX), BF16),
            jax.ShapeDtypeStruct((1, 1, 3), F32),
        ),
        in_specs=[hbm] * 10,
        out_specs=(vmem, vmem),
        scratch_shapes=[
            pltpu.VMEM((1, 1, TOK, D), BF16),
            pltpu.VMEM((1, 1, 2, SLOTS), jnp.int32),
            pltpu.VMEM((1, 1), jnp.int32),
            pltpu.VMEM((12, 1, IMAGES), F32),
            pltpu.VMEM((D,), F32),
            pltpu.VMEM((D,), F32),
            pltpu.VMEM((D, WIDTH + D), BF16),
            pltpu.VMEM((D, OUT + HALF), BF16),
            pltpu.VMEM((WIDTH, D), BF16),
            pltpu.VMEM((IMAGES, 2 * TOK, HALF), BF16),
            pltpu.VMEM((SIDE, SIDE, 128), F32),
            pltpu.VMEM((SIDE, SIDE, 128), F32),
            pltpu.VMEM((IMAGES * TOK, WIDTH), BF16),
            pltpu.VMEM((IMAGES * TOK, PIX), F32),
            pltpu.VMEM((4, IMAGES * TOK, 128), F32),
            pltpu.VMEM((IMAGES * TOK, 128), F32),
            pltpu.VMEM((IMAGES, 1, 128), F32),
            pltpu.VMEM((IMAGES, 1, 128), F32),
            dma((2, 17)),
            dma((2, 17)),
            dma((2, SIDE)),
            dma((2, SIDE)),
            dma((2, SIDE)),
            dma((2, SIDE)),
            dma((1,)),
            dma((1,)),
            dma((11,)),
        ],
        compiler_params=pltpu.CompilerParams(
            collective_id=0, has_side_effects=True, vmem_limit_bytes=64 * 1024 * 1024
        ),
    )(
        tokens, jnp.swapaxes(pair_list, 2, 3), pair_count, jnp.transpose(poses, (2, 0, 1)),
        gain_query, gain_kv, w_kv, w_query, w_out, w_head,
    )


def solution(mesh):
    return jax.shard_map(
        on_device,
        mesh=mesh,
        in_specs=(
            P("scene", "img", None, None),
            P("scene", "img", None, None),
            P("scene", "img"),
            P("scene", None, None),
            P(),
            P(),
            P("scene", None),
            P("scene", None),
            P("scene", None),
            P("scene", None),
        ),
        out_specs=(P("scene", "img", None, None), P("scene", "img", None)),
        check_vma=False,
    )
```
